32 devices in a mesh: grp: 2 (over y), sec: 4 (over z), mpo: 4 (over x, core).
Axes of the slice: x: 2, y: 2, z: 4, core: 2. Of those that a mesh axis runs over, the one named last changes fastest.
Arguments:
- psi: bfloat16 [64, 128, 3, 128], P(('grp', 'sec')), parts along dimension 0, may hold values from -6 to 6
- left_env: bfloat16 [16, 32, 128, 128], P(('grp', 'mpo'), 'sec'), parts along dimension 0, may hold values from -0.5 to 0.5
- right_env: bfloat16 [16, 32, 128, 128], P(('grp', 'mpo'), 'sec'), parts along dimension 0, may hold values from -0.1875 to 0.1875
- site_op: bfloat16 [16, 32, 3, 3], P(('grp', 'mpo'), 'sec'), parts along dimension 0, may hold values from -3.5 to 3.5
- source: int32 [4, 32], P('mpo'), may hold values from 0 to 31, as said below
Outputs:
- product: bfloat16 [128, 64, 3, 128], P('mpo', ('grp', 'sec')), parts along dimension 1
The draws below stay inside these ranges and needn't reach their ends.
There are 2 independent parts, one for each index of `grp`. The reference program is written for one: setup_inputs(seed, part) draws one part's arguments, and reference() takes and returns one part's arrays. A program takes and returns all parts, laid end to end along the dimension named above; an argument that names none is the same for every part. Nothing has to cross between parts.
Inputs may be any that keep to these rules, and one draw needn't show every extreme that they name: `source`: within each bond-charge group g and each aligned block of 8 output sectors, at most 2 entries name input sectors of one aligned block of 8 input sectors, and exactly 2 do for some block.
All inputs are finite; a program needn't handle non-finite values.
Results may differ from the reference program's by a relative error of at most 0.0058.
Values may be sent and summed in bfloat16 or wider, within the bound.
No kernel may reach another device: no remote copies, remote signals or barrier semaphores. Data moves between devices by JAX's collectives and lax.ppermute only.
A program may use at most 64 MiB of HBM per device.

```python
import jax
import jax.numpy as jnp
from jax import lax

BLK = 128
PH = 3
W_DEV = 2
S_DEV = 8
GROUPS = 4
W = 8
S = 32
CAP = 2
N_SEC = 4


def draw_source(key, part):
    key = jax.random.fold_in(key, 7)
    count = GROUPS * N_SEC
    first, second, third = jax.random.split(key, 3)
    orders = jax.vmap(lambda k: jax.random.permutation(k, N_SEC))(jax.random.split(first, count))
    senders = orders[:, jnp.arange(S_DEV) // CAP]
    shuffled = jax.vmap(lambda k, row: jax.random.permutation(k, row))(jax.random.split(second, count), senders)
    within = jax.random.randint(third, (count, S_DEV), 0, S_DEV)
    return (shuffled * S_DEV + within).reshape(GROUPS, S).astype(jnp.int32)


def block_scale(own_key, extent, cuts, least, top_value):
    gain = 1.0
    for dim, parts in cuts:
        draws = jax.random.uniform(jax.random.fold_in(jax.random.fold_in(own_key, 6), dim), (parts,), jnp.float32, least / len(cuts), top_value / len(cuts))
        gain = gain * jnp.repeat(jnp.exp(draws), extent[dim] // parts).reshape((-1,) + (1,) * (len(extent) - 1 - dim))
    return gain


def gaussian(rng, shape, scale, most, pieces=(), held_as=jnp.bfloat16):
    gain = block_scale(rng, shape, pieces, -0.22, 0.18) if pieces else 1.0
    drawn = jax.random.normal(rng, shape, jnp.float32) * scale * gain
    return jnp.minimum(jnp.maximum(drawn, -most), most).astype(held_as)


def setup_inputs(seed: int = 0, part: int = 0) -> dict:
    streams_of = jax.random.split(jax.random.key(seed), 6)
    part_splits = jax.random.split(jax.random.fold_in(streams_of[5], part), 6)
    psi = gaussian(part_splits[0], (S, BLK, PH, BLK), 1.0, 6.0, ((0, 4),))
    left_env = gaussian(part_splits[1], (W, S, BLK, BLK), BLK ** -0.5, 0.5, ((0, 4), (1, 4)))
    right_env = gaussian(part_splits[2], (W, S, BLK, BLK), (BLK * W) ** -0.5, 0.1875, ((0, 4), (1, 4)))
    site_op = gaussian(part_splits[3], (W, S, PH, PH), PH ** -0.5, 3.5, ((0, 4), (1, 4)))
    source = draw_source(jax.random.fold_in(streams_of[5], 71), part)
    return {"psi": psi, "left_env": left_env, "right_env": right_env, "site_op": site_op, "source": source}


def reference(psi, left_env, right_env, site_op, source):
    def one_index(acc, widx):
        group = widx // W_DEV
        rows = lax.dynamic_index_in_dim(source, group, 0, keepdims=False)
        taken = jnp.take(psi, rows, axis=0).astype(jnp.float32)
        lmat = lax.dynamic_index_in_dim(left_env, widx, 0, keepdims=False).astype(jnp.float32)
        rmat = lax.dynamic_index_in_dim(right_env, widx, 0, keepdims=False).astype(jnp.float32)
        opmat = lax.dynamic_index_in_dim(site_op, widx, 0, keepdims=False).astype(jnp.float32)
        left = jnp.einsum("tab,tbpc->tapc", lmat, taken).astype(jnp.bfloat16)
        mixed = jnp.einsum("tapc,tpq->taqc", left.astype(jnp.float32), opmat).astype(jnp.bfloat16)
        term = jnp.einsum("taqc,tcd->atqd", mixed.astype(jnp.float32), rmat)
        return acc + term, None

    start = jnp.zeros((BLK, S, PH, BLK), jnp.float32)
    total, unused = lax.scan(one_index, start, jnp.arange(W, dtype=jnp.int32))
    return total.astype(jnp.bfloat16)
```

```python
import functools

import jax
import jax.numpy as jnp
from jax import lax
from jax.experimental import pallas as pl
from jax.experimental.pallas import tpu as pltpu
from jax.sharding import PartitionSpec as P

SLOTS = 2
VMEM_BYTES = 8 * 1024 * 1024


def space(kind):
    return pl.BlockSpec(memory_space=kind)


def params():
    return pltpu.CompilerParams(vmem_limit_bytes=VMEM_BYTES)


def pick(table, base, count, block):
    zero = jnp.int32(0)
    seen, places, rows = zero, [zero, zero], [zero, zero]
    for t in range(count):
        value = table[0, base + t]
        owner = lax.div(value, jnp.int32(count))
        hit = owner == block
        row = value - owner * count
        for j in range(SLOTS):
            here = hit & (seen == j)
            places[j] = jnp.where(here, jnp.int32(t), places[j])
            rows[j] = jnp.where(here, row, rows[j])
        seen = seen + hit.astype(jnp.int32)
    return places, rows


def route_kernel(nsec, sdev, table, psi, *refs):
    outs, order, sems = refs[: nsec - 1], refs[nsec - 1], refs[nsec]
    me = lax.axis_index("sec")
    copies = []
    for k in range(1, nsec):
        other = jnp.bitwise_xor(me, k)
        rows = pick(table, other * sdev, sdev, me)[1]
        for j in range(SLOTS):
            copy = pltpu.make_async_copy(psi.at[rows[j]], outs[k - 1].at[j], sems.at[k - 1, j])
            copy.start()
            copies.append(copy)
    for k in range(nsec):
        places, rows = pick(table, me * sdev, sdev, jnp.bitwise_xor(me, k))
        for j in range(SLOTS):
            order[k * SLOTS + j] = places[j]
            if k == 0:
                order[nsec * SLOTS + j] = rows[j]
    for copy in copies:
        copy.wait()


def route(table, psi, nsec, sdev):
    block = psi.shape[1:]
    shapes = [jax.ShapeDtypeStruct((SLOTS,) + block, psi.dtype)] * (nsec - 1)
    shapes.append(jax.ShapeDtypeStruct((nsec * SLOTS + SLOTS,), jnp.int32))
    return pl.pallas_call(
        functools.partial(route_kernel, nsec, sdev),
        out_shape=shapes,
        in_specs=[space(pltpu.SMEM), space(pl.ANY)],
        out_specs=[space(pl.ANY)] * (nsec - 1) + [space(pltpu.SMEM)],
        scratch_shapes=[pltpu.SemaphoreType.DMA((nsec - 1, SLOTS))],
        compiler_params=params(),
        name="route",
    )(table, psi)


def apply_kernel(classes, nsec, nmpo, order, ops, *refs):
    ncls = len(classes)
    blocks, left, right = refs[:ncls], refs[ncls], refs[ncls + 1]
    keep = refs[ncls + 2]
    sends = refs[ncls + 3 : ncls + 2 + nmpo]
    xbuf, lbuf, rbuf, sems = refs[ncls + 2 + nmpo :]
    wdev, sdev, blk = left.shape[0], left.shape[1], left.shape[2]
    phys = xbuf.shape[1]
    part = blk // nmpo
    me = lax.axis_index("mpo")
    places, copies = [], []
    for i, k in enumerate(classes):
        for j in range(SLOTS):
            s = i * SLOTS + j
            t = order[k * SLOTS + j]
            row = order[nsec * SLOTS + j] if k == 0 else j
            places.append(t)
            mine = [
                pltpu.make_async_copy(blocks[i].at[row], xbuf.at[s], sems.at[s, 0]),
                pltpu.make_async_copy(left.at[:, t], lbuf.at[s], sems.at[s, 1]),
                pltpu.make_async_copy(right.at[:, t], rbuf.at[s], sems.at[s, 2]),
            ]
            for copy in mine:
                copy.start()
            copies.append(mine)
    for s in range(ncls * SLOTS):
        for copy in copies[s]:
            copy.wait()
        rows = []
        for w in range(wdev):
            for m in range(nmpo):
                start = pl.multiple_of(jnp.bitwise_xor(me, m) * part, part)
                rows.append(lbuf[s, w, pl.ds(start, part), :])
        lhs = jnp.concatenate(rows, axis=0)
        lefts = []
        for p in range(phys):
            done = jnp.dot(lhs, xbuf[s, p], preferred_element_type=jnp.float32)
            lefts.append(done.astype(jnp.bfloat16).astype(jnp.float32))
        mixed = []
        for q in range(phys):
            across = []
            for w in range(wdev):
                base = ((w * sdev) + places[s]) * (phys * phys) + q
                total = None
                for p in range(phys):
                    term = lefts[p][w * blk : (w + 1) * blk] * ops[base + p * phys]
                    total = term if total is None else total + term
                across.append(total.astype(jnp.bfloat16))
            mixed.append(jnp.concatenate(across, axis=1))
        rmat = rbuf[s].reshape(wdev * blk, blk)
        for q in range(phys):
            out = jnp.dot(mixed[q], rmat, preferred_element_type=jnp.float32)
            keep[s, q] = out[:part]
            for m in range(1, nmpo):
                sends[m - 1][s, q] = out[m * part : (m + 1) * part].astype(jnp.bfloat16)


def apply(classes, order, ops, blocks, left, right, nsec, nmpo):
    wdev, sdev, blk = left.shape[:3]
    phys = blocks[0].shape[1]
    n = len(classes) * SLOTS
    piece = (n, phys, blk // nmpo, blk)
    shapes = [jax.ShapeDtypeStruct(piece, jnp.float32)]
    shapes += [jax.ShapeDtypeStruct(piece, jnp.bfloat16)] * (nmpo - 1)
    return pl.pallas_call(
        functools.partial(apply_kernel, classes, nsec, nmpo),
        out_shape=shapes,
        in_specs=[space(pltpu.SMEM)] * 2 + [space(pl.ANY)] * (len(classes) + 2),
        out_specs=[space(pltpu.VMEM)] * nmpo,
        scratch_shapes=[
            pltpu.VMEM((n, phys, blk, blk), jnp.bfloat16),
            pltpu.VMEM((n, wdev, blk, blk), jnp.bfloat16),
            pltpu.VMEM((n, wdev, blk, blk), jnp.bfloat16),
            pltpu.SemaphoreType.DMA((n, 3)),
        ],
        compiler_params=params(),
        cost_estimate=pl.CostEstimate(
            flops=n * wdev * phys * blk**3 * 4,
            bytes_accessed=n * (phys + 2 * wdev) * blk * blk * 2,
            transcendentals=0,
        ),
        name="apply",
    )(order, ops, *blocks, left, right)


def merge_kernel(groups, nmpo, *refs):
    orders = refs[:nmpo]
    stages = refs[nmpo : nmpo + len(groups) * nmpo]
    out, acc = refs[-2], refs[-1]
    for m in range(nmpo):
        for g, classes in enumerate(groups):
            got = stages[g * nmpo + m]
            for i, k in enumerate(classes):
                for j in range(SLOTS):
                    t = orders[m][k * SLOTS + j]
                    value = got[i * SLOTS + j].astype(jnp.float32)
                    acc[t] = value if m == 0 else acc[t] + value
    for q in range(out.shape[1]):
        out[:, q] = jnp.swapaxes(acc[:, q], 0, 1).astype(out.dtype)


def merge(groups, orders, stages, sdev):
    nmpo = len(orders)
    phys, part, blk = stages[0][0].shape[1:]
    flat = [array for stage in stages for array in stage]
    return pl.pallas_call(
        functools.partial(merge_kernel, groups, nmpo),
        out_shape=jax.ShapeDtypeStruct((part, phys, sdev, blk), jnp.bfloat16),
        in_specs=[space(pltpu.SMEM)] * nmpo + [space(pltpu.VMEM)] * len(flat),
        out_specs=space(pltpu.VMEM),
        scratch_shapes=[pltpu.VMEM((sdev, phys, part, blk), jnp.float32)],
        compiler_params=params(),
        name="merge",
    )(*orders, *flat)


def fast_shards(psi, left_env, right_env, site_op, source):
    nsec = lax.axis_size("sec")
    nmpo = lax.axis_size("mpo")
    sdev = psi.shape[0]
    blocks = jnp.transpose(psi, (0, 2, 1, 3))
    ops = site_op.astype(jnp.float32).reshape(-1)
    routed = route(source, blocks, nsec, sdev)
    outgoing, order = routed[:-1], routed[-1]
    arrived = [blocks]
    for k in range(1, nsec):
        arrived.append(lax.ppermute(outgoing[k - 1], "sec", [(i, i ^ k) for i in range(nsec)]))

    def across(value, m):
        return lax.ppermute(value, "mpo", [(i, i ^ m) for i in range(nmpo)])

    orders = [order] + [across(order, m) for m in range(1, nmpo)]
    groups = [tuple(range(0, nsec - 2)), (nsec - 2,), (nsec - 1,)]
    stages = []
    for classes in groups:
        parts = apply(
            classes, order, ops, [arrived[k] for k in classes], left_env, right_env, nsec, nmpo
        )
        stages.append([parts[0]] + [across(parts[m], m) for m in range(1, nmpo)])
    out = merge(groups, orders, stages, sdev)
    return jnp.transpose(out, (0, 2, 1, 3))


def any_shards(psi, left_env, right_env, site_op, source):
    me_sec = lax.axis_index("sec")
    nsec = lax.axis_size("sec")
    sdev = psi.shape[0]
    blk = psi.shape[1]
    phys = psi.shape[2]
    slots = max(2, (sdev + nsec - 1) // nsec)
    table = source[0]
    owners = (table // sdev).reshape(nsec, sdev)
    mine = owners == me_sec
    ranked = jnp.cumsum(mine.astype(jnp.int32), axis=1) - 1
    picked = mine[:, None, :] & (
        ranked[:, None, :] == jnp.arange(slots, dtype=jnp.int32)[None, :, None]
    )
    local_rows = (table % sdev).reshape(nsec, sdev)
    chosen = jnp.sum(jnp.where(picked, local_rows[:, None, :], 0), axis=2)
    outgoing = jnp.take(psi, chosen.reshape(-1), axis=0).reshape(nsec, slots, blk, phys, blk)
    arrived = lax.all_to_all(outgoing, "sec", split_axis=0, concat_axis=0, tiled=True)
    my_sources = lax.dynamic_slice_in_dim(table, me_sec * sdev, sdev)
    sender = my_sources // sdev
    onehot = (sender[:, None] == jnp.arange(nsec, dtype=jnp.int32)[None, :]).astype(jnp.int32)
    slot_index = jnp.sum(jnp.cumsum(onehot, axis=0) * onehot, axis=1) - 1
    position = sender * slots + slot_index
    taken = jnp.take(arrived.reshape(nsec * slots, blk, phys, blk), position, axis=0)
    left = jnp.einsum(
        "wtab,tbpc->wtapc", left_env, taken, preferred_element_type=jnp.float32
    ).astype(jnp.bfloat16)
    mixed = jnp.einsum(
        "wtapc,wtpq->wtaqc", left, site_op, preferred_element_type=jnp.float32
    ).astype(jnp.bfloat16)
    partial_value = jnp.einsum(
        "wtaqc,wtcd->atqd", mixed, right_env, preferred_element_type=jnp.float32
    )
    summed = lax.psum_scatter(partial_value, "mpo", scatter_dimension=0, tiled=True)
    return summed.astype(jnp.bfloat16)


def shards(psi, left_env, right_env, site_op, source):
    nsec = lax.axis_size("sec")
    nmpo = lax.axis_size("mpo")
    exact = psi.shape[0] == SLOTS * nsec and nsec == 4 and nmpo == 4
    body = fast_shards if exact else any_shards
    return body(psi, left_env, right_env, site_op, source)


def solution(mesh):
    placed = (
        P(("grp", "sec"), None, None, None),
        P(("grp", "mpo"), "sec", None, None),
        P(("grp", "mpo"), "sec", None, None),
        P(("grp", "mpo"), "sec", None, None),
        P("mpo", None),
    )
    return jax.shard_map(
        shards,
        mesh=mesh,
        in_specs=placed,
        out_specs=P("mpo", ("grp", "sec"), None, None),
        check_vma=False,
    )
```

```python
import functools

import jax
import jax.numpy as jnp
from jax import lax
from jax.experimental import pallas as pl
from jax.experimental.pallas import tpu as pltpu
from jax.sharding import PartitionSpec as P

SLOTS = 2
EARLY = 2
VMEM_BYTES = 16 * 1024 * 1024


def space(kind):
    return pl.BlockSpec(memory_space=kind)


def params():
    return pltpu.CompilerParams(vmem_limit_bytes=VMEM_BYTES)


def split(value, count):
    if count & (count - 1) == 0:
        shift = count.bit_length() - 1
        return jnp.right_shift(value, shift), jnp.bitwise_and(value, count - 1)
    owner = lax.div(value, jnp.int32(count))
    return owner, value - owner * count


def pick(table, base, count, block):
    zero = jnp.int32(0)
    seen, places, rows = zero, [zero, zero], [zero, zero]
    for t in range(count):
        owner, row = split(table[0, base + t], count)
        hit = owner == block
        for j in range(SLOTS):
            here = hit & (seen == j)
            places[j] = jnp.where(here, jnp.int32(t), places[j])
            rows[j] = jnp.where(here, row, rows[j])
        seen = seen + hit.astype(jnp.int32)
    return places, rows


def route_kernel(nsec, sdev, source, psi, *refs):
    outs, order, table, load, sems = refs[: nsec - 1], *refs[nsec - 1 :]
    me = lax.axis_index("sec")
    fetch = pltpu.make_async_copy(source, table, load)
    fetch.start()
    fetch.wait()
    copies = []
    for k in range(1, nsec):
        other = jnp.bitwise_xor(me, k)
        rows = pick(table, other * sdev, sdev, me)[1]
        for j in range(SLOTS):
            copy = pltpu.make_async_copy(psi.at[rows[j]], outs[k - 1].at[j], sems.at[k - 1, j])
            copy.start()
            copies.append(copy)
    for k in range(nsec):
        places, rows = pick(table, me * sdev, sdev, jnp.bitwise_xor(me, k))
        for j in range(SLOTS):
            order[k * SLOTS + j] = places[j]
            if k == 0:
                order[nsec * SLOTS + j] = rows[j]
    for copy in copies:
        copy.wait()


def route(source, psi, nsec, sdev):
    block = psi.shape[1:]
    shapes = [jax.ShapeDtypeStruct((SLOTS,) + block, psi.dtype)] * (nsec - 1)
    shapes.append(jax.ShapeDtypeStruct((nsec * SLOTS + SLOTS,), jnp.int32))
    return pl.pallas_call(
        functools.partial(route_kernel, nsec, sdev),
        out_shape=shapes,
        in_specs=[space(pltpu.HBM), space(pltpu.HBM)],
        out_specs=[space(pl.ANY)] * (nsec - 1) + [space(pltpu.SMEM)],
        scratch_shapes=[
            pltpu.SMEM(source.shape, jnp.int32),
            pltpu.SemaphoreType.DMA,
            pltpu.SemaphoreType.DMA((nsec - 1, SLOTS)),
        ],
        compiler_params=params(),
        name="route",
    )(source, psi)


def product(lhs, block, rhs, ops, base, wdev, phys):
    rows = lhs.shape[0] // wdev
    lefts = []
    for p in range(phys):
        done = jnp.dot(lhs, block[p], preferred_element_type=jnp.float32)
        lefts.append(done.astype(jnp.bfloat16).astype(jnp.float32))
    outs = []
    for q in range(phys):
        across = []
        for w in range(wdev):
            total = None
            for p in range(phys):
                term = lefts[p][w * rows : (w + 1) * rows] * ops[base[w] + p * phys + q]
                total = term if total is None else total + term
            across.append(total.astype(jnp.bfloat16))
        mixed = jnp.concatenate(across, axis=1)
        outs.append(jnp.dot(mixed, rhs, preferred_element_type=jnp.float32))
    return outs


def op_base(t, wdev, sdev, phys):
    return [(w * sdev + t) * (phys * phys) for w in range(wdev)]


def early_kernel(nsec, nmpo, order, ops, psi, near_block, left, right, *refs):
    far_keep, far_give, near_keep, near_give, lfar, lnear, rstage, local, sems = refs
    wdev, sdev, blk = left.shape[:3]
    phys = local.shape[1]
    part = blk // nmpo
    me = lax.axis_index("mpo")
    copies = []
    for j in range(SLOTS):
        copy = pltpu.make_async_copy(psi.at[order[nsec * SLOTS + j]], local.at[j], sems.at[j])
        copy.start()
        copies.append(copy)

    def rows(w, t, m):
        start = pl.multiple_of(jnp.bitwise_xor(me, m) * part, part)
        return left[w, t, pl.ds(start, part), :]

    for s in range((nsec - EARLY) * SLOTS):
        t = order[EARLY * SLOTS + s]
        lfar[s] = jnp.concatenate([rows(w, t, m) for w in range(wdev) for m in (2, 3)], axis=0)
        lnear[s] = jnp.concatenate([rows(w, t, m) for w in range(wdev) for m in (0, 1)], axis=0)
        rstage[s] = right[:, t].reshape(wdev * blk, blk)
    for copy in copies:
        copy.wait()
    for k in (1, 0):
        for j in range(SLOTS):
            s = k * SLOTS + j
            t = order[s]
            lhs = jnp.concatenate(
                [rows(w, t, m) for w in range(wdev) for m in (2, 3, 0, 1)], axis=0
            )
            rhs = right[:, t].reshape(wdev * blk, blk)
            source = near_block if k == 1 else local
            block = [source[j, p] for p in range(phys)]
            outs = product(lhs, block, rhs, ops, op_base(t, wdev, sdev, phys), wdev, phys)
            for q in range(phys):
                far_keep[s, q] = outs[q][:part]
                far_give[s, q] = outs[q][part : 2 * part].astype(jnp.bfloat16)
                near_keep[s, q] = outs[q][2 * part : 3 * part]
                near_give[s, q] = outs[q][3 * part :].astype(jnp.bfloat16)


def early(order, ops, psi, near_block, left, right, nsec, nmpo):
    wdev, sdev, blk = left.shape[:3]
    phys = psi.shape[1]
    part = blk // nmpo
    n, late_n = EARLY * SLOTS, (nsec - EARLY) * SLOTS
    keep = jax.ShapeDtypeStruct((n, phys, part, blk), jnp.float32)
    give = jax.ShapeDtypeStruct((n, phys, part, blk), jnp.bfloat16)
    half = jax.ShapeDtypeStruct((late_n, wdev * 2 * part, blk), jnp.bfloat16)
    whole = jax.ShapeDtypeStruct((late_n, wdev * blk, blk), jnp.bfloat16)
    return pl.pallas_call(
        functools.partial(early_kernel, nsec, nmpo),
        out_shape=[keep, give, keep, give, half, half, whole],
        in_specs=[space(pltpu.SMEM)] * 2 + [space(pltpu.HBM)] + [space(pltpu.VMEM)] * 3,
        out_specs=[space(pltpu.VMEM)] * 7,
        scratch_shapes=[
            pltpu.VMEM((SLOTS, phys, blk, blk), jnp.bfloat16),
            pltpu.SemaphoreType.DMA((SLOTS,)),
        ],
        compiler_params=params(),
        cost_estimate=pl.CostEstimate(
            flops=n * wdev * phys * blk**3 * 4,
            bytes_accessed=8 * 1024 * 1024,
            transcendentals=0,
        ),
        name="early",
    )(order, ops, psi, near_block, left, right)


def late_kernel(nsec, wdev, sdev, order, ops, *refs):
    nlate = nsec - EARLY
    blocks, (lside, rstage, early_keep, early_give, keep, give) = refs[:nlate], refs[nlate:]
    phys, part = keep.shape[1], keep.shape[2]
    for s in range(EARLY * SLOTS):
        t = order[s]
        keep[t] = early_keep[s]
        give[t] = early_give[s]
    for s in range(nlate * SLOTS):
        t = order[EARLY * SLOTS + s]
        block = [blocks[s // SLOTS][s % SLOTS, p] for p in range(phys)]
        base = op_base(t, wdev, sdev, phys)
        outs = product(lside[s], block, rstage[s], ops, base, wdev, phys)
        for q in range(phys):
            keep[t, q] = outs[q][:part]
            give[t, q] = outs[q][part:].astype(jnp.bfloat16)


def late(order, ops, blocks, lside, rstage, early_keep, early_give, nsec, wdev, sdev):
    phys, part, blk = early_keep.shape[1:]
    n = len(blocks) * SLOTS
    return pl.pallas_call(
        functools.partial(late_kernel, nsec, wdev, sdev),
        out_shape=[
            jax.ShapeDtypeStruct((sdev, phys, part, blk), jnp.float32),
            jax.ShapeDtypeStruct((sdev, phys, part, blk), jnp.bfloat16),
        ],
        in_specs=[space(pltpu.SMEM)] * 2 + [space(pltpu.VMEM)] * (len(blocks) + 4),
        out_specs=[space(pltpu.VMEM)] * 2,
        compiler_params=params(),
        cost_estimate=pl.CostEstimate(
            flops=n * wdev * phys * blk**3 * 2,
            bytes_accessed=4 * 1024 * 1024,
            transcendentals=0,
        ),
        name="late",
    )(order, ops, *blocks, lside, rstage, early_keep, early_give)


def pair_kernel(keep, got, out):
    out[...] = (keep[...] + got[...].astype(jnp.float32)).astype(out.dtype)


def pair(keep, got):
    return pl.pallas_call(
        pair_kernel,
        out_shape=jax.ShapeDtypeStruct(got.shape, got.dtype),
        in_specs=[space(pltpu.VMEM)] * 2,
        out_specs=space(pltpu.VMEM),
        compiler_params=params(),
        name="pair",
    )(keep, got)


def finish_kernel(keep, near, far, out):
    for q in range(out.shape[1]):
        total = keep[:, q] + near[:, q].astype(jnp.float32) + far[:, q].astype(jnp.float32)
        out[:, q] = jnp.swapaxes(total, 0, 1).astype(out.dtype)


def finish(keep, near, far):
    sdev, phys, part, blk = keep.shape
    return pl.pallas_call(
        finish_kernel,
        out_shape=jax.ShapeDtypeStruct((part, phys, sdev, blk), jnp.bfloat16),
        in_specs=[space(pltpu.VMEM)] * 3,
        out_specs=space(pltpu.VMEM),
        compiler_params=params(),
        name="finish",
    )(keep, near, far)


def fast_shards(psi, left_env, right_env, site_op, source):
    nsec = lax.axis_size("sec")
    nmpo = lax.axis_size("mpo")
    sdev = psi.shape[0]
    wdev = left_env.shape[0]
    blocks = jnp.transpose(psi, (0, 2, 1, 3))
    ops = site_op.astype(jnp.float32).reshape(-1)
    routed = route(source, blocks, nsec, sdev)
    outgoing, order = routed[:-1], routed[-1]
    arrived = []
    for k in range(1, nsec):
        arrived.append(lax.ppermute(outgoing[k - 1], "sec", [(i, i ^ k) for i in range(nsec)]))

    def across(value, m):
        return lax.ppermute(value, "mpo", [(i, i ^ m) for i in range(nmpo)])

    far_keep, far_give, near_keep, near_give, lfar, lnear, rstage = early(
        order, ops, blocks, arrived[0], left_env, right_env, nsec, nmpo
    )
    rest = arrived[1:]
    keep_far, give_far = late(order, ops, rest, lfar, rstage, far_keep, far_give, nsec, wdev, sdev)
    over = across(pair(keep_far, across(give_far, 1)), 2)
    keep_near, give_near = late(
        order, ops, rest, lnear, rstage, near_keep, near_give, nsec, wdev, sdev
    )
    out = finish(keep_near, across(give_near, 1), over)
    return jnp.transpose(out, (0, 2, 1, 3))


def any_shards(psi, left_env, right_env, site_op, source):
    me_sec = lax.axis_index("sec")
    nsec = lax.axis_size("sec")
    sdev = psi.shape[0]
    blk = psi.shape[1]
    phys = psi.shape[2]
    slots = max(2, (sdev + nsec - 1) // nsec)
    table = source[0]
    owners = (table // sdev).reshape(nsec, sdev)
    mine = owners == me_sec
    ranked = jnp.cumsum(mine.astype(jnp.int32), axis=1) - 1
    picked = mine[:, None, :] & (
        ranked[:, None, :] == jnp.arange(slots, dtype=jnp.int32)[None, :, None]
    )
    local_rows = (table % sdev).reshape(nsec, sdev)
    chosen = jnp.sum(jnp.where(picked, local_rows[:, None, :], 0), axis=2)
    outgoing = jnp.take(psi, chosen.reshape(-1), axis=0).reshape(nsec, slots, blk, phys, blk)
    arrived = lax.all_to_all(outgoing, "sec", split_axis=0, concat_axis=0, tiled=True)
    my_sources = lax.dynamic_slice_in_dim(table, me_sec * sdev, sdev)
    sender = my_sources // sdev
    onehot = (sender[:, None] == jnp.arange(nsec, dtype=jnp.int32)[None, :]).astype(jnp.int32)
    slot_index = jnp.sum(jnp.cumsum(onehot, axis=0) * onehot, axis=1) - 1
    position = sender * slots + slot_index
    taken = jnp.take(arrived.reshape(nsec * slots, blk, phys, blk), position, axis=0)
    left = jnp.einsum(
        "wtab,tbpc->wtapc", left_env, taken, preferred_element_type=jnp.float32
    ).astype(jnp.bfloat16)
    mixed = jnp.einsum(
        "wtapc,wtpq->wtaqc", left, site_op, preferred_element_type=jnp.float32
    ).astype(jnp.bfloat16)
    partial_value = jnp.einsum(
        "wtaqc,wtcd->atqd", mixed, right_env, preferred_element_type=jnp.float32
    )
    summed = lax.psum_scatter(partial_value, "mpo", scatter_dimension=0, tiled=True)
    return summed.astype(jnp.bfloat16)


def shards(psi, left_env, right_env, site_op, source):
    nsec = lax.axis_size("sec")
    nmpo = lax.axis_size("mpo")
    exact = psi.shape[0] == SLOTS * nsec and nsec == 4 and nmpo == 4
    body = fast_shards if exact else any_shards
    return body(psi, left_env, right_env, site_op, source)


def solution(mesh):
    placed = (
        P(("grp", "sec"), None, None, None),
        P(("grp", "mpo"), "sec", None, None),
        P(("grp", "mpo"), "sec", None, None),
        P(("grp", "mpo"), "sec", None, None),
        P("mpo", None),
    )
    return jax.shard_map(
        shards,
        mesh=mesh,
        in_specs=placed,
        out_specs=P("mpo", ("grp", "sec"), None, None),
        check_vma=False,
    )
```

```python
import functools

import jax
import jax.numpy as jnp
from jax import lax
from jax.experimental import pallas as pl
from jax.experimental.pallas import tpu as pltpu
from jax.sharding import PartitionSpec as P

SLOTS = 2
EARLY = 2
VMEM_BYTES = 16 * 1024 * 1024


def space(kind):
    return pl.BlockSpec(memory_space=kind)


def params():
    return pltpu.CompilerParams(vmem_limit_bytes=VMEM_BYTES)


def split(value, count):
    if count & (count - 1) == 0:
        shift = count.bit_length() - 1
        return jnp.right_shift(value, shift), jnp.bitwise_and(value, count - 1)
    owner = lax.div(value, jnp.int32(count))
    return owner, value - owner * count


def pick(table, base, count, block):
    zero = jnp.int32(0)
    seen, places, rows = zero, [zero, zero], [zero, zero]
    for t in range(count):
        owner, row = split(table[0, base + t], count)
        hit = owner == block
        for j in range(SLOTS):
            here = hit & (seen == j)
            places[j] = jnp.where(here, jnp.int32(t), places[j])
            rows[j] = jnp.where(here, row, rows[j])
        seen = seen + hit.astype(jnp.int32)
    return places, rows


def route_kernel(classes, sdev, source, psi, *refs):
    outs, (table, load, sems) = refs[: len(classes)], refs[len(classes) :]
    me = lax.axis_index("sec")
    fetch = pltpu.make_async_copy(source, table, load)
    fetch.start()
    fetch.wait()
    copies = []
    for i, k in enumerate(classes):
        other = jnp.bitwise_xor(me, k)
        rows = pick(table, other * sdev, sdev, me)[1]
        for j in range(SLOTS):
            copy = pltpu.make_async_copy(psi.at[rows[j]], outs[i].at[j], sems.at[i, j])
            copy.start()
            copies.append(copy)
    for copy in copies:
        copy.wait()


def route(classes, source, psi):
    block = psi.shape[1:]
    return pl.pallas_call(
        functools.partial(route_kernel, classes, psi.shape[0]),
        out_shape=[jax.ShapeDtypeStruct((SLOTS,) + block, psi.dtype)] * len(classes),
        in_specs=[space(pl.ANY)] * 2,
        out_specs=[space(pl.ANY)] * len(classes),
        scratch_shapes=[
            pltpu.SMEM(source.shape, jnp.int32),
            pltpu.SemaphoreType.DMA,
            pltpu.SemaphoreType.DMA((len(classes), SLOTS)),
        ],
        compiler_params=params(),
        name="route",
    )(source, psi)


def order_kernel(nsec, sdev, source, after, order, table, load):
    me = lax.axis_index("sec")
    fetch = pltpu.make_async_copy(source, table, load)
    fetch.start()
    fetch.wait()
    for k in range(nsec):
        places, rows = pick(table, me * sdev, sdev, jnp.bitwise_xor(me, k))
        for j in range(SLOTS):
            order[k * SLOTS + j] = places[j]
            if k == 0:
                order[nsec * SLOTS + j] = rows[j]


def receive_order(source, after, nsec, sdev):
    return pl.pallas_call(
        functools.partial(order_kernel, nsec, sdev),
        out_shape=jax.ShapeDtypeStruct((nsec * SLOTS + SLOTS,), jnp.int32),
        in_specs=[space(pl.ANY)] * 2,
        out_specs=space(pltpu.SMEM),
        scratch_shapes=[pltpu.SMEM(source.shape, jnp.int32), pltpu.SemaphoreType.DMA],
        compiler_params=params(),
        name="order",
    )(source, after)


def product(lhs, block, rhs, ops, base, wdev, phys):
    rows = lhs.shape[0] // wdev
    blk = block[0].shape[1]
    wide = jnp.dot(lhs, jnp.concatenate(block, axis=1), preferred_element_type=jnp.float32)
    wide = wide.astype(jnp.bfloat16).astype(jnp.float32)
    lefts = [wide[:, p * blk : (p + 1) * blk] for p in range(phys)]
    outs = []
    for q in range(phys):
        across = []
        for w in range(wdev):
            total = None
            for p in range(phys):
                term = lefts[p][w * rows : (w + 1) * rows] * ops[base[w] + p * phys + q]
                total = term if total is None else total + term
            across.append(total.astype(jnp.bfloat16))
        mixed = jnp.concatenate(across, axis=1)
        outs.append(jnp.dot(mixed, rhs, preferred_element_type=jnp.float32))
    return outs


def op_base(t, wdev, sdev, phys):
    return [(w * sdev + t) * (phys * phys) for w in range(wdev)]


QUARTERS = (2, 0, 3, 1)


def early_kernel(nsec, nmpo, order, ops, psi, near_block, left, right, *refs):
    keep, far_give, near_give, lstage, rstage, local, sems = refs
    wdev, sdev, blk = left.shape[:3]
    phys = local.shape[1]
    part = blk // nmpo
    me = lax.axis_index("mpo")
    copies = []
    for j in range(SLOTS):
        copy = pltpu.make_async_copy(psi.at[order[nsec * SLOTS + j]], local.at[j], sems.at[j])
        copy.start()
        copies.append(copy)

    def side(t):
        rows = []
        for w in range(wdev):
            for m in QUARTERS:
                start = pl.multiple_of(jnp.bitwise_xor(me, m) * part, part)
                rows.append(left[w, t, pl.ds(start, part), :])
        return jnp.concatenate(rows, axis=0)

    for s in range((nsec - EARLY) * SLOTS):
        t = order[EARLY * SLOTS + s]
        lstage[s] = side(t)
        rstage[s] = right[:, t].reshape(wdev * blk, blk)
    for copy in copies:
        copy.wait()
    for k in (1, 0):
        for j in range(SLOTS):
            s = k * SLOTS + j
            t = order[s]
            rhs = right[:, t].reshape(wdev * blk, blk)
            source = near_block if k == 1 else local
            block = [source[j, p] for p in range(phys)]
            outs = product(side(t), block, rhs, ops, op_base(t, wdev, sdev, phys), wdev, phys)
            for q in range(phys):
                keep[0, s, q] = outs[q][:part]
                keep[1, s, q] = outs[q][part : 2 * part]
                far_give[s, q] = outs[q][2 * part : 3 * part].astype(jnp.bfloat16)
                near_give[s, q] = outs[q][3 * part :].astype(jnp.bfloat16)


def early(order, ops, psi, near_block, left, right, nsec, nmpo):
    wdev, sdev, blk = left.shape[:3]
    phys = psi.shape[1]
    part = blk // nmpo
    n, late_n = EARLY * SLOTS, (nsec - EARLY) * SLOTS
    keep = jax.ShapeDtypeStruct((2, n, phys, part, blk), jnp.float32)
    give = jax.ShapeDtypeStruct((n, phys, part, blk), jnp.bfloat16)
    whole = jax.ShapeDtypeStruct((late_n, wdev * blk, blk), jnp.bfloat16)
    return pl.pallas_call(
        functools.partial(early_kernel, nsec, nmpo),
        out_shape=[keep, give, give, whole, whole],
        in_specs=[space(pltpu.SMEM)] * 2 + [space(pl.ANY)] + [space(pltpu.VMEM)] * 3,
        out_specs=[space(pltpu.VMEM)] * 5,
        scratch_shapes=[
            pltpu.VMEM((SLOTS, phys, blk, blk), jnp.bfloat16),
            pltpu.SemaphoreType.DMA((SLOTS,)),
        ],
        compiler_params=params(),
        cost_estimate=pl.CostEstimate(
            flops=n * wdev * phys * blk**3 * 4,
            bytes_accessed=8 * 1024 * 1024,
            transcendentals=0,
        ),
        name="early",
    )(order, ops, psi, near_block, left, right)


def late_kernel(nsec, wdev, sdev, order, ops, *refs):
    nlate = nsec - EARLY
    blocks, refs = refs[:nlate], refs[nlate:]
    lstage, rstage, early_keep, early_far, early_near, keep, far_give, near_give = refs
    phys, part = far_give.shape[1], far_give.shape[2]
    for s in range(EARLY * SLOTS):
        t = order[s]
        for side in range(2):
            keep[side, t] = early_keep[side, s]
        far_give[t] = early_far[s]
        near_give[t] = early_near[s]
    for s in range(nlate * SLOTS):
        t = order[EARLY * SLOTS + s]
        block = [blocks[s // SLOTS][s % SLOTS, p] for p in range(phys)]
        base = op_base(t, wdev, sdev, phys)
        outs = product(lstage[s], block, rstage[s], ops, base, wdev, phys)
        for q in range(phys):
            keep[0, t, q] = outs[q][:part]
            keep[1, t, q] = outs[q][part : 2 * part]
            far_give[t, q] = outs[q][2 * part : 3 * part].astype(jnp.bfloat16)
            near_give[t, q] = outs[q][3 * part :].astype(jnp.bfloat16)


def late(order, ops, blocks, staged, nsec, wdev, sdev):
    phys, part, blk = staged[0].shape[2:]
    n = len(blocks) * SLOTS
    give = jax.ShapeDtypeStruct((sdev, phys, part, blk), jnp.bfloat16)
    return pl.pallas_call(
        functools.partial(late_kernel, nsec, wdev, sdev),
        out_shape=[jax.ShapeDtypeStruct((2, sdev, phys, part, blk), jnp.float32), give, give],
        in_specs=[space(pltpu.SMEM)] * 2 + [space(pltpu.VMEM)] * (len(blocks) + 5),
        out_specs=[space(pltpu.VMEM)] * 3,
        compiler_params=params(),
        cost_estimate=pl.CostEstimate(
            flops=n * wdev * phys * blk**3 * 4,
            bytes_accessed=8 * 1024 * 1024,
            transcendentals=0,
        ),
        name="late",
    )(order, ops, *blocks, *staged[3:], *staged[:3])


def pair_kernel(keep, got, out):
    out[...] = (keep[0] + got[...].astype(jnp.float32)).astype(out.dtype)


def pair(keep, got):
    return pl.pallas_call(
        pair_kernel,
        out_shape=jax.ShapeDtypeStruct(got.shape, got.dtype),
        in_specs=[space(pltpu.VMEM)] * 2,
        out_specs=space(pltpu.VMEM),
        compiler_params=params(),
        name="pair",
    )(keep, got)


def finish_kernel(keep, near, far, out):
    for q in range(out.shape[1]):
        total = keep[1, :, q] + near[:, q].astype(jnp.float32) + far[:, q].astype(jnp.float32)
        out[:, q] = jnp.swapaxes(total, 0, 1).astype(out.dtype)


def finish(keep, near, far):
    sdev, phys, part, blk = far.shape
    return pl.pallas_call(
        finish_kernel,
        out_shape=jax.ShapeDtypeStruct((part, phys, sdev, blk), jnp.bfloat16),
        in_specs=[space(pltpu.VMEM)] * 3,
        out_specs=space(pltpu.VMEM),
        compiler_params=params(),
        name="finish",
    )(keep, near, far)


def fast_shards(psi, left_env, right_env, site_op, source):
    nsec = lax.axis_size("sec")
    nmpo = lax.axis_size("mpo")
    sdev = psi.shape[0]
    wdev = left_env.shape[0]
    blocks = jnp.transpose(psi, (0, 2, 1, 3))
    ops = site_op.astype(jnp.float32).reshape(-1)
    table = pltpu.with_memory_space_constraint(source, pltpu.HBM)
    outgoing = route(
        tuple(range(1, nsec)), table, pltpu.with_memory_space_constraint(blocks, pltpu.HBM)
    )
    order = receive_order(table, outgoing[0], nsec, sdev)
    arrived = []
    for k in range(1, nsec):
        arrived.append(lax.ppermute(outgoing[k - 1], "sec", [(i, i ^ k) for i in range(nsec)]))

    def across(value, m):
        return lax.ppermute(value, "mpo", [(i, i ^ m) for i in range(nmpo)])

    staged = early(order, ops, blocks, arrived[0], left_env, right_env, nsec, nmpo)
    keep, far_give, near_give = late(order, ops, arrived[1:], staged, nsec, wdev, sdev)
    over = across(pair(keep, across(far_give, 1)), 2)
    out = finish(keep, across(near_give, 1), over)
    return jnp.transpose(out, (0, 2, 1, 3))


def any_shards(psi, left_env, right_env, site_op, source):
    me_sec = lax.axis_index("sec")
    nsec = lax.axis_size("sec")
    sdev = psi.shape[0]
    blk = psi.shape[1]
    phys = psi.shape[2]
    slots = max(2, (sdev + nsec - 1) // nsec)
    table = source[0]
    owners = (table // sdev).reshape(nsec, sdev)
    mine = owners == me_sec
    ranked = jnp.cumsum(mine.astype(jnp.int32), axis=1) - 1
    picked = mine[:, None, :] & (
        ranked[:, None, :] == jnp.arange(slots, dtype=jnp.int32)[None, :, None]
    )
    local_rows = (table % sdev).reshape(nsec, sdev)
    chosen = jnp.sum(jnp.where(picked, local_rows[:, None, :], 0), axis=2)
    outgoing = jnp.take(psi, chosen.reshape(-1), axis=0).reshape(nsec, slots, blk, phys, blk)
    arrived = lax.all_to_all(outgoing, "sec", split_axis=0, concat_axis=0, tiled=True)
    my_sources = lax.dynamic_slice_in_dim(table, me_sec * sdev, sdev)
    sender = my_sources // sdev
    onehot = (sender[:, None] == jnp.arange(nsec, dtype=jnp.int32)[None, :]).astype(jnp.int32)
    slot_index = jnp.sum(jnp.cumsum(onehot, axis=0) * onehot, axis=1) - 1
    position = sender * slots + slot_index
    taken = jnp.take(arrived.reshape(nsec * slots, blk, phys, blk), position, axis=0)
    left = jnp.einsum(
        "wtab,tbpc->wtapc", left_env, taken, preferred_element_type=jnp.float32
    ).astype(jnp.bfloat16)
    mixed = jnp.einsum(
        "wtapc,wtpq->wtaqc", left, site_op, preferred_element_type=jnp.float32
    ).astype(jnp.bfloat16)
    partial_value = jnp.einsum(
        "wtaqc,wtcd->atqd", mixed, right_env, preferred_element_type=jnp.float32
    )
    summed = lax.psum_scatter(partial_value, "mpo", scatter_dimension=0, tiled=True)
    return summed.astype(jnp.bfloat16)


def shards(psi, left_env, right_env, site_op, source):
    nsec = lax.axis_size("sec")
    nmpo = lax.axis_size("mpo")
    exact = psi.shape[0] == SLOTS * nsec and nsec == 4 and nmpo == 4
    body = fast_shards if exact else any_shards
    return body(psi, left_env, right_env, site_op, source)


def solution(mesh):
    placed = (
        P(("grp", "sec"), None, None, None),
        P(("grp", "mpo"), "sec", None, None),
        P(("grp", "mpo"), "sec", None, None),
        P(("grp", "mpo"), "sec", None, None),
        P("mpo", None),
    )
    return jax.shard_map(
        shards,
        mesh=mesh,
        in_specs=placed,
        out_specs=P("mpo", ("grp", "sec"), None, None),
        check_vma=False,
    )
```

```python
import functools

import jax
import jax.numpy as jnp
from jax import lax
from jax.experimental import pallas as pl
from jax.experimental.pallas import tpu as pltpu
from jax.sharding import PartitionSpec as P

SLOTS = 2
EARLY = (0,)
LATE = (2, 1, 3)
VMEM_BYTES = 16 * 1024 * 1024


def space(kind):
    return pl.BlockSpec(memory_space=kind)


def params():
    return pltpu.CompilerParams(vmem_limit_bytes=VMEM_BYTES)


def split(value, count):
    if count & (count - 1) == 0:
        shift = count.bit_length() - 1
        return jnp.right_shift(value, shift), jnp.bitwise_and(value, count - 1)
    owner = lax.div(value, jnp.int32(count))
    return owner, value - owner * count


def pick(table, base, count, block):
    zero = jnp.int32(0)
    seen, places, rows = zero, [zero, zero], [zero, zero]
    for t in range(count):
        owner, row = split(table[0, base + t], count)
        hit = owner == block
        for j in range(SLOTS):
            here = hit & (seen == j)
            places[j] = jnp.where(here, jnp.int32(t), places[j])
            rows[j] = jnp.where(here, row, rows[j])
        seen = seen + hit.astype(jnp.int32)
    return places, rows


def route_kernel(nsec, source, psi, *refs):
    outs, (table, held, load, sems) = refs[:nsec], refs[nsec:]
    sdev = psi.shape[0]
    me = lax.axis_index("sec")
    fetch = pltpu.make_async_copy(source, table, load)
    fetch.start()
    copies = []
    for row in range(sdev):
        copy = pltpu.make_async_copy(psi.at[row], held.at[row], sems.at[row])
        copy.start()
        copies.append(copy)
    fetch.wait()
    rows = [pick(table, jnp.bitwise_xor(me, k) * sdev, sdev, me)[1] for k in range(nsec)]
    for copy in copies:
        copy.wait()
    for k in range(nsec):
        for j in range(SLOTS):
            outs[k][j] = held[rows[k][j]]


def route(source, psi, nsec):
    block = psi.shape[1:]
    return pl.pallas_call(
        functools.partial(route_kernel, nsec),
        out_shape=[jax.ShapeDtypeStruct((SLOTS,) + block, psi.dtype)] * nsec,
        in_specs=[space(pl.ANY)] * 2,
        out_specs=[space(pltpu.VMEM)] * nsec,
        scratch_shapes=[
            pltpu.SMEM(source.shape, jnp.int32),
            pltpu.VMEM(psi.shape, psi.dtype),
            pltpu.SemaphoreType.DMA,
            pltpu.SemaphoreType.DMA((psi.shape[0],)),
        ],
        compiler_params=params(),
        name="route",
    )(source, psi)


def order_kernel(nsec, sdev, source, after, order, table, load):
    me = lax.axis_index("sec")
    fetch = pltpu.make_async_copy(source, table, load)
    fetch.start()
    fetch.wait()
    for k in range(nsec):
        places = pick(table, me * sdev, sdev, jnp.bitwise_xor(me, k))[0]
        for j in range(SLOTS):
            order[k * SLOTS + j] = places[j]


def receive_order(source, after, nsec, sdev):
    return pl.pallas_call(
        functools.partial(order_kernel, nsec, sdev),
        out_shape=jax.ShapeDtypeStruct((nsec * SLOTS,), jnp.int32),
        in_specs=[space(pl.ANY)] * 2,
        out_specs=space(pltpu.SMEM),
        scratch_shapes=[pltpu.SMEM(source.shape, jnp.int32), pltpu.SemaphoreType.DMA],
        compiler_params=params(),
        name="order",
    )(source, after)


def left_rows(lhs, block):
    wide = jnp.dot(lhs, jnp.concatenate(block, axis=1), preferred_element_type=jnp.float32)
    return wide.astype(jnp.bfloat16)


def right_rows(wide, rhs, ops, base, wdev, phys):
    rows = wide.shape[0] // wdev
    blk = rhs.shape[1]
    outs = []
    for q in range(phys):
        across = []
        for w in range(wdev):
            total = None
            for p in range(phys):
                part = wide[w * rows : (w + 1) * rows, p * blk : (p + 1) * blk]
                term = part.astype(jnp.float32) * ops[base[w] + p * phys + q]
                total = term if total is None else total + term
            across.append(total.astype(jnp.bfloat16))
        mixed = jnp.concatenate(across, axis=1)
        outs.append(jnp.dot(mixed, rhs, preferred_element_type=jnp.float32))
    return outs


def product(lhs, block, rhs, ops, base, wdev, phys):
    return right_rows(left_rows(lhs, block), rhs, ops, base, wdev, phys)


def op_base(t, wdev, sdev, phys):
    return [(w * sdev + t) * (phys * phys) for w in range(wdev)]


QUARTERS = (2, 0, 3, 1)


def early_kernel(nsec, nmpo, order, ops, *refs):
    blocks, refs = refs[: len(EARLY)], refs[len(EARLY) :]
    left, right, keep, far_give, near_give, lstage, rstage = refs
    wdev, sdev, blk = left.shape[:3]
    phys = blocks[0].shape[1]
    part = blk // nmpo
    me = lax.axis_index("mpo")

    def side(t):
        rows = []
        for w in range(wdev):
            for m in QUARTERS:
                start = pl.multiple_of(jnp.bitwise_xor(me, m) * part, part)
                rows.append(left[w, t, pl.ds(start, part), :])
        return jnp.concatenate(rows, axis=0)

    for s in range(len(LATE) * SLOTS):
        t = order[LATE[s // SLOTS] * SLOTS + s % SLOTS]
        lstage[s] = side(t)
        rstage[s] = right[:, t].reshape(wdev * blk, blk)
    for i, k in enumerate(EARLY):
        for j in range(SLOTS):
            s = i * SLOTS + j
            t = order[k * SLOTS + j]
            rhs = right[:, t].reshape(wdev * blk, blk)
            block = [blocks[i][j, p] for p in range(phys)]
            outs = product(side(t), block, rhs, ops, op_base(t, wdev, sdev, phys), wdev, phys)
            for q in range(phys):
                keep[0, s, q] = outs[q][:part]
                keep[1, s, q] = outs[q][part : 2 * part]
                far_give[s, q] = outs[q][2 * part : 3 * part].astype(jnp.bfloat16)
                near_give[s, q] = outs[q][3 * part :].astype(jnp.bfloat16)


def early(order, ops, blocks, left, right, nsec, nmpo):
    wdev, sdev, blk = left.shape[:3]
    phys = blocks[0].shape[1]
    part = blk // nmpo
    n, late_n = len(EARLY) * SLOTS, len(LATE) * SLOTS
    keep = jax.ShapeDtypeStruct((2, n, phys, part, blk), jnp.float32)
    give = jax.ShapeDtypeStruct((n, phys, part, blk), jnp.bfloat16)
    whole = jax.ShapeDtypeStruct((late_n, wdev * blk, blk), jnp.bfloat16)
    return pl.pallas_call(
        functools.partial(early_kernel, nsec, nmpo),
        out_shape=[keep, give, give, whole, whole],
        in_specs=[space(pltpu.SMEM)] * 2 + [space(pltpu.VMEM)] * (len(EARLY) + 2),
        out_specs=[space(pltpu.VMEM)] * 5,
        compiler_params=params(),
        cost_estimate=pl.CostEstimate(
            flops=n * wdev * phys * blk**3 * 4,
            bytes_accessed=8 * 1024 * 1024,
            transcendentals=0,
        ),
        name="early",
    )(order, ops, *blocks, left, right)


def late_kernel(nsec, wdev, sdev, order_in, ops_in, *refs):
    nlate = len(LATE)
    blocks, refs = refs[:nlate], refs[nlate:]
    lstage, rstage, early_keep, early_far, early_near, keep, far_give, near_give = refs[:8]
    order, ops, sems = refs[8:]
    phys, part = far_give.shape[1], far_give.shape[2]
    loads = [
        pltpu.make_async_copy(order_in, order, sems.at[0]),
        pltpu.make_async_copy(ops_in, ops, sems.at[1]),
    ]
    for load in loads:
        load.start()
    wides = []
    for s in range(nlate * SLOTS):
        block = [blocks[s // SLOTS][s % SLOTS, p] for p in range(phys)]
        wides.append(left_rows(lstage[s], block))
    for load in loads:
        load.wait()
    for s in range(nlate * SLOTS):
        t = order[LATE[s // SLOTS] * SLOTS + s % SLOTS]
        base = op_base(t, wdev, sdev, phys)
        outs = right_rows(wides[s], rstage[s], ops, base, wdev, phys)
        for q in range(phys):
            keep[0, t, q] = outs[q][:part]
            keep[1, t, q] = outs[q][part : 2 * part]
            far_give[t, q] = outs[q][2 * part : 3 * part].astype(jnp.bfloat16)
            near_give[t, q] = outs[q][3 * part :].astype(jnp.bfloat16)
    for s in range(len(EARLY) * SLOTS):
        t = order[EARLY[s // SLOTS] * SLOTS + s % SLOTS]
        for side in range(2):
            keep[side, t] = early_keep[side, s]
        far_give[t] = early_far[s]
        near_give[t] = early_near[s]


def late(order, ops, blocks, staged, nsec, wdev, sdev):
    phys, part, blk = staged[0].shape[2:]
    n = len(blocks) * SLOTS
    give = jax.ShapeDtypeStruct((sdev, phys, part, blk), jnp.bfloat16)
    return pl.pallas_call(
        functools.partial(late_kernel, nsec, wdev, sdev),
        out_shape=[jax.ShapeDtypeStruct((2, sdev, phys, part, blk), jnp.float32), give, give],
        in_specs=[space(pl.ANY)] * 2 + [space(pltpu.VMEM)] * (len(blocks) + 5),
        out_specs=[space(pltpu.VMEM)] * 3,
        scratch_shapes=[
            pltpu.SMEM(order.shape, order.dtype),
            pltpu.SMEM(ops.shape, ops.dtype),
            pltpu.SemaphoreType.DMA((2,)),
        ],
        compiler_params=params(),
        cost_estimate=pl.CostEstimate(
            flops=n * wdev * phys * blk**3 * 4,
            bytes_accessed=8 * 1024 * 1024,
            transcendentals=0,
        ),
        name="late",
    )(order, ops, *blocks, *staged[3:], *staged[:3])


def pair_kernel(keep, got, out):
    out[...] = (keep[0] + got[...].astype(jnp.float32)).astype(out.dtype)


def pair(keep, got):
    return pl.pallas_call(
        pair_kernel,
        out_shape=jax.ShapeDtypeStruct(got.shape, got.dtype),
        in_specs=[space(pltpu.VMEM)] * 2,
        out_specs=space(pltpu.VMEM),
        compiler_params=params(),
        name="pair",
    )(keep, got)


def finish_kernel(keep, near, far, out):
    for q in range(out.shape[1]):
        total = keep[1, :, q] + near[:, q].astype(jnp.float32) + far[:, q].astype(jnp.float32)
        out[:, q] = jnp.swapaxes(total, 0, 1).astype(out.dtype)


def finish(keep, near, far):
    sdev, phys, part, blk = far.shape
    return pl.pallas_call(
        finish_kernel,
        out_shape=jax.ShapeDtypeStruct((part, phys, sdev, blk), jnp.bfloat16),
        in_specs=[space(pltpu.VMEM)] * 3,
        out_specs=space(pltpu.VMEM),
        compiler_params=params(),
        name="finish",
    )(keep, near, far)


def fast_shards(psi, left_env, right_env, site_op, source):
    nsec = lax.axis_size("sec")
    nmpo = lax.axis_size("mpo")
    sdev = psi.shape[0]
    wdev = left_env.shape[0]
    blocks = jnp.transpose(psi, (0, 2, 1, 3))
    ops = site_op.astype(jnp.float32).reshape(-1)
    table = pltpu.with_memory_space_constraint(source, pltpu.HBM)
    held = route(table, pltpu.with_memory_space_constraint(blocks, pltpu.HBM), nsec)
    order = receive_order(table, held[0], nsec, sdev)
    arrived = [held[0]]
    for k in range(1, nsec):
        arrived.append(lax.ppermute(held[k], "sec", [(i, i ^ k) for i in range(nsec)]))

    def across(value, m):
        return lax.ppermute(value, "mpo", [(i, i ^ m) for i in range(nmpo)])

    staged = early(order, ops, [arrived[k] for k in EARLY], left_env, right_env, nsec, nmpo)
    keep, far_give, near_give = late(order, ops, [arrived[k] for k in LATE], staged, nsec, wdev, sdev)
    far = across(pair(keep, across(far_give, 1)), 2)
    out = finish(keep, across(near_give, 1), far)
    return jnp.transpose(out, (0, 2, 1, 3))


def any_shards(psi, left_env, right_env, site_op, source):
    me_sec = lax.axis_index("sec")
    nsec = lax.axis_size("sec")
    sdev = psi.shape[0]
    blk = psi.shape[1]
    phys = psi.shape[2]
    slots = max(2, (sdev + nsec - 1) // nsec)
    table = source[0]
    owners = (table // sdev).reshape(nsec, sdev)
    mine = owners == me_sec
    ranked = jnp.cumsum(mine.astype(jnp.int32), axis=1) - 1
    picked = mine[:, None, :] & (
        ranked[:, None, :] == jnp.arange(slots, dtype=jnp.int32)[None, :, None]
    )
    local_rows = (table % sdev).reshape(nsec, sdev)
    chosen = jnp.sum(jnp.where(picked, local_rows[:, None, :], 0), axis=2)
    outgoing = jnp.take(psi, chosen.reshape(-1), axis=0).reshape(nsec, slots, blk, phys, blk)
    arrived = lax.all_to_all(outgoing, "sec", split_axis=0, concat_axis=0, tiled=True)
    my_sources = lax.dynamic_slice_in_dim(table, me_sec * sdev, sdev)
    sender = my_sources // sdev
    onehot = (sender[:, None] == jnp.arange(nsec, dtype=jnp.int32)[None, :]).astype(jnp.int32)
    slot_index = jnp.sum(jnp.cumsum(onehot, axis=0) * onehot, axis=1) - 1
    position = sender * slots + slot_index
    taken = jnp.take(arrived.reshape(nsec * slots, blk, phys, blk), position, axis=0)
    left = jnp.einsum(
        "wtab,tbpc->wtapc", left_env, taken, preferred_element_type=jnp.float32
    ).astype(jnp.bfloat16)
    mixed = jnp.einsum(
        "wtapc,wtpq->wtaqc", left, site_op, preferred_element_type=jnp.float32
    ).astype(jnp.bfloat16)
    partial_value = jnp.einsum(
        "wtaqc,wtcd->atqd", mixed, right_env, preferred_element_type=jnp.float32
    )
    summed = lax.psum_scatter(partial_value, "mpo", scatter_dimension=0, tiled=True)
    return summed.astype(jnp.bfloat16)


def shards(psi, left_env, right_env, site_op, source):
    nsec = lax.axis_size("sec")
    nmpo = lax.axis_size("mpo")
    exact = psi.shape[0] == SLOTS * nsec and nsec == 4 and nmpo == 4
    body = fast_shards if exact else any_shards
    return body(psi, left_env, right_env, site_op, source)


def solution(mesh):
    placed = (
        P(("grp", "sec"), None, None, None),
        P(("grp", "mpo"), "sec", None, None),
        P(("grp", "mpo"), "sec", None, None),
        P(("grp", "mpo"), "sec", None, None),
        P("mpo", None),
    )
    return jax.shard_map(
        shards,
        mesh=mesh,
        in_specs=placed,
        out_specs=P("mpo", ("grp", "sec"), None, None),
        check_vma=False,
    )
```

```python
import functools

import jax
import jax.numpy as jnp
from jax import lax
from jax.experimental import pallas as pl
from jax.experimental.pallas import tpu as pltpu
from jax.sharding import PartitionSpec as P

SLOTS = 2
EARLY = (0,)
MID = (2, 1)
LAST = 3
LATE = MID + (LAST,)
NAME_ROWS = 16
VMEM_BYTES = 16 * 1024 * 1024


def space(kind):
    return pl.BlockSpec(memory_space=kind)


def params():
    return pltpu.CompilerParams(vmem_limit_bytes=VMEM_BYTES)


def split(value, count):
    if count & (count - 1) == 0:
        shift = count.bit_length() - 1
        return jnp.right_shift(value, shift), jnp.bitwise_and(value, count - 1)
    owner = lax.div(value, jnp.int32(count))
    return owner, value - owner * count


def pick(table, base, count, block):
    zero = jnp.int32(0)
    seen, places, rows = zero, [zero, zero], [zero, zero]
    for t in range(count):
        owner, row = split(table[0, base + t], count)
        hit = owner == block
        for j in range(SLOTS):
            here = hit & (seen == j)
            places[j] = jnp.where(here, jnp.int32(t), places[j])
            rows[j] = jnp.where(here, row, rows[j])
        seen = seen + hit.astype(jnp.int32)
    return places, rows


def route_kernel(classes, source, psi, *refs):
    outs, (table, held, load, sems) = refs[: len(classes)], refs[len(classes) :]
    sdev = psi.shape[0]
    me = lax.axis_index("sec")
    fetch = pltpu.make_async_copy(source, table, load)
    fetch.start()
    copies = []
    for row in range(sdev):
        copy = pltpu.make_async_copy(psi.at[row], held.at[row], sems.at[row])
        copy.start()
        copies.append(copy)
    fetch.wait()
    rows = [pick(table, jnp.bitwise_xor(me, k) * sdev, sdev, me)[1] for k in classes]
    for copy in copies:
        copy.wait()
    for i in range(len(classes)):
        for j in range(SLOTS):
            outs[i][j] = held[rows[i][j]]


def route(classes, source, psi):
    block = psi.shape[1:]
    return pl.pallas_call(
        functools.partial(route_kernel, classes),
        out_shape=[jax.ShapeDtypeStruct((SLOTS,) + block, psi.dtype)] * len(classes),
        in_specs=[space(pl.ANY)] * 2,
        out_specs=[space(pltpu.VMEM)] * len(classes),
        scratch_shapes=[
            pltpu.SMEM(source.shape, jnp.int32),
            pltpu.VMEM(psi.shape, psi.dtype),
            pltpu.SemaphoreType.DMA,
            pltpu.SemaphoreType.DMA((psi.shape[0],)),
        ],
        compiler_params=params(),
        name="route",
    )(source, psi)


def double_kernel(block, out, sems):
    copies = [pltpu.make_async_copy(block, out.at[i], sems.at[i]) for i in range(2)]
    for copy in copies:
        copy.start()
    for copy in copies:
        copy.wait()


def double(block):
    return pl.pallas_call(
        double_kernel,
        out_shape=jax.ShapeDtypeStruct((2,) + block.shape, block.dtype),
        in_specs=[space(pltpu.VMEM)],
        out_specs=space(pl.ANY),
        scratch_shapes=[pltpu.SemaphoreType.DMA((2,))],
        compiler_params=params(),
        name="double",
    )(block)


def order_kernel(nsec, sdev, source, after, order, table, load):
    me = lax.axis_index("sec")
    fetch = pltpu.make_async_copy(source, table, load)
    fetch.start()
    fetch.wait()
    for k in range(nsec):
        places = pick(table, me * sdev, sdev, jnp.bitwise_xor(me, k))[0]
        for j in range(SLOTS):
            order[k * SLOTS + j] = places[j]


def receive_order(source, after, nsec, sdev):
    return pl.pallas_call(
        functools.partial(order_kernel, nsec, sdev),
        out_shape=jax.ShapeDtypeStruct((nsec * SLOTS,), jnp.int32),
        in_specs=[space(pl.ANY)] * 2,
        out_specs=space(pltpu.SMEM),
        scratch_shapes=[pltpu.SMEM(source.shape, jnp.int32), pltpu.SemaphoreType.DMA],
        compiler_params=params(),
        name="order",
    )(source, after)


def left_rows(lhs, block):
    wide = jnp.dot(lhs, jnp.concatenate(block, axis=1), preferred_element_type=jnp.float32)
    return wide.astype(jnp.bfloat16)


def right_rows(wide, rhs, op, wdev, phys):
    rows = wide.shape[0] // wdev
    blk = rhs.shape[1]
    outs = []
    for q in range(phys):
        across = []
        for w in range(wdev):
            total = None
            for p in range(phys):
                part = wide[w * rows : (w + 1) * rows, p * blk : (p + 1) * blk]
                term = part.astype(jnp.float32) * op(w, p, q)
                total = term if total is None else total + term
            across.append(total.astype(jnp.bfloat16))
        mixed = jnp.concatenate(across, axis=1)
        outs.append(jnp.dot(mixed, rhs, preferred_element_type=jnp.float32))
    return outs


def scalar_op(ops, t, sdev, phys):
    return lambda w, p, q: ops[(w * sdev + t) * (phys * phys) + p * phys + q]


def row_op(rows, s, phys):
    def op(w, p, q):
        i = (w * phys + p) * phys + q
        return rows[s, i : i + 1, :]

    return op


QUARTERS = (2, 0, 3, 1)


def early_kernel(nsec, nmpo, order, ops, *refs):
    blocks, refs = refs[: len(EARLY)], refs[len(EARLY) :]
    left, right, keep, far_give, near_give, lstage, rstage, oprows, named = refs
    wdev, sdev, blk = left.shape[:3]
    phys = blocks[0].shape[1]
    part = blk // nmpo
    me = lax.axis_index("mpo")

    def side(t):
        rows = []
        for w in range(wdev):
            for m in QUARTERS:
                start = pl.multiple_of(jnp.bitwise_xor(me, m) * part, part)
                rows.append(left[w, t, pl.ds(start, part), :])
        return jnp.concatenate(rows, axis=0)

    for s in range(len(LATE) * SLOTS):
        t = order[LATE[s // SLOTS] * SLOTS + s % SLOTS]
        lstage[s] = side(t)
        rstage[s] = right[:, t].reshape(wdev * blk, blk)
    for s in range(SLOTS):
        t = order[LAST * SLOTS + s]
        named[s] = jnp.full(named.shape[1:], t.astype(jnp.float32), jnp.float32).astype(named.dtype)
        op = scalar_op(ops, t, sdev, phys)
        for w in range(wdev):
            for p in range(phys):
                for q in range(phys):
                    i = (w * phys + p) * phys + q
                    oprows[s, i : i + 1, :] = jnp.full((1, blk), op(w, p, q), jnp.float32)
    for i, k in enumerate(EARLY):
        for j in range(SLOTS):
            s = i * SLOTS + j
            t = order[k * SLOTS + j]
            rhs = right[:, t].reshape(wdev * blk, blk)
            block = [blocks[i][j, p] for p in range(phys)]
            op = scalar_op(ops, t, sdev, phys)
            outs = right_rows(left_rows(side(t), block), rhs, op, wdev, phys)
            for q in range(phys):
                keep[0, s, q] = outs[q][:part]
                keep[1, s, q] = outs[q][part : 2 * part]
                far_give[s, q] = outs[q][2 * part : 3 * part].astype(jnp.bfloat16)
                near_give[s, q] = outs[q][3 * part :].astype(jnp.bfloat16)


def early(order, ops, blocks, left, right, nsec, nmpo):
    wdev, sdev, blk = left.shape[:3]
    phys = blocks[0].shape[1]
    part = blk // nmpo
    n, late_n = len(EARLY) * SLOTS, len(LATE) * SLOTS
    keep = jax.ShapeDtypeStruct((2, n, phys, part, blk), jnp.float32)
    give = jax.ShapeDtypeStruct((n, phys, part, blk), jnp.bfloat16)
    rows = jax.ShapeDtypeStruct((SLOTS, wdev * phys * phys, blk), jnp.float32)
    name = jax.ShapeDtypeStruct((SLOTS, NAME_ROWS, blk), jnp.bfloat16)
    whole = jax.ShapeDtypeStruct((late_n, wdev * blk, blk), jnp.bfloat16)
    return pl.pallas_call(
        functools.partial(early_kernel, nsec, nmpo),
        out_shape=[keep, give, give, whole, whole, rows, name],
        in_specs=[space(pltpu.SMEM)] * 2 + [space(pltpu.VMEM)] * (len(EARLY) + 2),
        out_specs=[space(pltpu.VMEM)] * 7,
        compiler_params=params(),
        cost_estimate=pl.CostEstimate(
            flops=n * wdev * phys * blk**3 * 4,
            bytes_accessed=8 * 1024 * 1024,
            transcendentals=0,
        ),
        name="early",
    )(order, ops, *blocks, left, right)


def mid_kernel(wdev, sdev, order_in, ops_in, *refs):
    nmid = len(MID)
    blocks, refs = refs[:nmid], refs[nmid:]
    lstage, rstage, early_keep, early_far, early_near, keep, far_give, near_give = refs[:8]
    order, ops, sems = refs[8:]
    phys, part = far_give.shape[1], far_give.shape[2]
    loads = [
        pltpu.make_async_copy(order_in, order, sems.at[0]),
        pltpu.make_async_copy(ops_in, ops, sems.at[1]),
    ]
    for load in loads:
        load.start()
    wides = []
    for s in range(nmid * SLOTS):
        block = [blocks[s // SLOTS][s % SLOTS, p] for p in range(phys)]
        wides.append(left_rows(lstage[s], block))
    for load in loads:
        load.wait()

    def place(classes, s):
        return order[classes[s // SLOTS] * SLOTS + s % SLOTS]

    for s in range(nmid * SLOTS):
        t = place(MID, s)
        outs = right_rows(wides[s], rstage[s], scalar_op(ops, t, sdev, phys), wdev, phys)
        for q in range(phys):
            keep[0, t, q] = outs[q][:part]
            keep[1, t, q] = outs[q][part : 2 * part]
            far_give[t, q] = outs[q][2 * part : 3 * part].astype(jnp.bfloat16)
            near_give[t, q] = outs[q][3 * part :].astype(jnp.bfloat16)
    for s in range(len(EARLY) * SLOTS):
        t = place(EARLY, s)
        for side in range(2):
            keep[side, t] = early_keep[side, s]
        far_give[t] = early_far[s]
        near_give[t] = early_near[s]
    for s in range(SLOTS):
        t = order[LAST * SLOTS + s]
        for side in range(2):
            keep[side, t] = jnp.zeros(keep.shape[2:], keep.dtype)
        far_give[t] = jnp.zeros(far_give.shape[1:], far_give.dtype)
        near_give[t] = jnp.zeros(near_give.shape[1:], near_give.dtype)


def mid(order, ops, blocks, staged, wdev, sdev):
    phys, part, blk = staged[0].shape[2:]
    n = len(blocks) * SLOTS
    give = jax.ShapeDtypeStruct((sdev, phys, part, blk), jnp.bfloat16)
    return pl.pallas_call(
        functools.partial(mid_kernel, wdev, sdev),
        out_shape=[jax.ShapeDtypeStruct((2, sdev, phys, part, blk), jnp.float32), give, give],
        in_specs=[space(pl.ANY)] * 2 + [space(pltpu.VMEM)] * (len(blocks) + 5),
        out_specs=[space(pltpu.VMEM)] * 3,
        scratch_shapes=[
            pltpu.SMEM(order.shape, order.dtype),
            pltpu.SMEM(ops.shape, ops.dtype),
            pltpu.SemaphoreType.DMA((2,)),
        ],
        compiler_params=params(),
        cost_estimate=pl.CostEstimate(
            flops=n * wdev * phys * blk**3 * 4,
            bytes_accessed=8 * 1024 * 1024,
            transcendentals=0,
        ),
        name="mid",
    )(order, ops, *blocks, *staged[3:5], *staged[:3])


def last_kernel(wdev, after, block, lstage, rstage, oprows, named, *gives):
    phys, blk = block.shape[2], block.shape[4]
    part = blk // len(gives)
    first = len(MID) * SLOTS
    me = lax.axis_index("sec")
    other = (jnp.bitwise_xor(me, LAST) > me).astype(jnp.int32)
    wides = []
    for s in range(SLOTS):
        wides.append(left_rows(lstage[first + s], [block[other, s, p] for p in range(phys)]))
    for s in range(SLOTS):
        outs = right_rows(wides[s], rstage[first + s], row_op(oprows, s, phys), wdev, phys)
        for i, m in enumerate(QUARTERS):
            for q in range(phys):
                rows = outs[q][i * part : (i + 1) * part].astype(gives[m].dtype)
                gives[m][s, q * part : (q + 1) * part] = rows
            gives[m][s, phys * part :] = named[s].astype(gives[m].dtype)


def last(after, block, staged, wdev):
    phys, part, blk = staged[0].shape[2:]
    shape = (SLOTS, phys * part + NAME_ROWS, blk)
    give = jax.ShapeDtypeStruct(shape, jnp.bfloat16)
    return pl.pallas_call(
        functools.partial(last_kernel, wdev),
        out_shape=[jax.ShapeDtypeStruct(shape, jnp.float32)] + [give] * 3,
        in_specs=[space(pl.ANY)] + [space(pltpu.VMEM)] * 5,
        out_specs=[space(pltpu.VMEM)] * 4,
        compiler_params=params(),
        cost_estimate=pl.CostEstimate(
            flops=SLOTS * wdev * phys * blk**3 * 4,
            bytes_accessed=4 * 1024 * 1024,
            transcendentals=0,
        ),
        name="last",
    )(after, block, *staged[3:])


def pair_kernel(keep, got, out):
    out[...] = (keep[0] + got[...].astype(jnp.float32)).astype(out.dtype)


def pair(keep, got):
    return pl.pallas_call(
        pair_kernel,
        out_shape=jax.ShapeDtypeStruct(got.shape, got.dtype),
        in_specs=[space(pltpu.VMEM)] * 2,
        out_specs=space(pltpu.VMEM),
        compiler_params=params(),
        name="pair",
    )(keep, got)


def tail_sum(tails, t):
    total = None
    for tail in tails:
        rows = tail.shape[1] - NAME_ROWS
        for s in range(SLOTS):
            here = tail[s, rows:, :].astype(jnp.float32)[:1] == t
            value = jnp.where(here, tail[s, :rows, :].astype(jnp.float32), 0.0)
            total = value if total is None else total + value
    return total


def base_kernel(keep, near, far, own, mate, acc):
    phys, part, blk = acc.shape[1:]
    for t in range(acc.shape[0]):
        total = keep[1, t] + near[t].astype(jnp.float32) + far[t].astype(jnp.float32)
        acc[t] = total + tail_sum((own, mate), t).reshape(phys, part, blk)


def base(keep, near, far, own, mate):
    return pl.pallas_call(
        base_kernel,
        out_shape=jax.ShapeDtypeStruct(far.shape, jnp.float32),
        in_specs=[space(pltpu.VMEM)] * 5,
        out_specs=space(pltpu.VMEM),
        compiler_params=params(),
        name="base",
    )(keep, near, far, own, mate)


def finish_kernel(total, tail2, tail3, out, acc):
    sdev, phys, part, blk = acc.shape
    for t in range(sdev):
        acc[t] = total[t] + tail_sum((tail2, tail3), t).reshape(phys, part, blk)
    for q in range(phys):
        out[:, q] = jnp.swapaxes(acc[:, q], 0, 1).astype(out.dtype)


def finish(total, tail2, tail3):
    sdev, phys, part, blk = total.shape
    return pl.pallas_call(
        finish_kernel,
        out_shape=jax.ShapeDtypeStruct((part, phys, sdev, blk), jnp.bfloat16),
        in_specs=[space(pltpu.VMEM)] * 3,
        out_specs=space(pltpu.VMEM),
        scratch_shapes=[pltpu.VMEM(total.shape, total.dtype)],
        compiler_params=params(),
        name="finish",
    )(total, tail2, tail3)


def fast_shards(psi, left_env, right_env, site_op, source):
    nsec = lax.axis_size("sec")
    nmpo = lax.axis_size("mpo")
    sdev = psi.shape[0]
    wdev = left_env.shape[0]
    blocks = jnp.transpose(psi, (0, 2, 1, 3))
    ops = site_op.astype(jnp.float32).reshape(-1)
    table = pltpu.with_memory_space_constraint(source, pltpu.HBM)
    pinned = pltpu.with_memory_space_constraint(blocks, pltpu.HBM)
    held = route(EARLY + MID + (LAST,), table, pinned)
    arrived = {0: held[0]}
    for k, value in zip(MID, held[len(EARLY) :]):
        arrived[k] = lax.ppermute(value, "sec", [(i, i ^ k) for i in range(nsec)])
    both = double(held[-1])
    order = receive_order(table, both, nsec, sdev)
    pairs = [[i, i ^ LAST] for i in range(nsec) if i < i ^ LAST]
    final = lax.all_to_all(both, "sec", 0, 0, axis_index_groups=pairs, tiled=True)

    def across(value, m):
        return lax.ppermute(value, "mpo", [(i, i ^ m) for i in range(nmpo)])

    staged = early(order, ops, [arrived[k] for k in EARLY], left_env, right_env, nsec, nmpo)
    keep, far_give, near_give = mid(order, ops, [arrived[k] for k in MID], staged, wdev, sdev)
    summed = pair(keep, across(far_give, 1))
    far = across(summed, 2)
    near = across(near_give, 1)
    own, give1, give2, give3 = last(summed, final, staged, wdev)
    total = base(keep, near, far, own, across(give1, 1))
    out = finish(total, across(give2, 2), across(give3, 3))
    return jnp.transpose(out, (0, 2, 1, 3))


def any_shards(psi, left_env, right_env, site_op, source):
    me_sec = lax.axis_index("sec")
    nsec = lax.axis_size("sec")
    sdev = psi.shape[0]
    blk = psi.shape[1]
    phys = psi.shape[2]
    slots = max(2, (sdev + nsec - 1) // nsec)
    table = source[0]
    owners = (table // sdev).reshape(nsec, sdev)
    mine = owners == me_sec
    ranked = jnp.cumsum(mine.astype(jnp.int32), axis=1) - 1
    picked = mine[:, None, :] & (
        ranked[:, None, :] == jnp.arange(slots, dtype=jnp.int32)[None, :, None]
    )
    local_rows = (table % sdev).reshape(nsec, sdev)
    chosen = jnp.sum(jnp.where(picked, local_rows[:, None, :], 0), axis=2)
    outgoing = jnp.take(psi, chosen.reshape(-1), axis=0).reshape(nsec, slots, blk, phys, blk)
    arrived = lax.all_to_all(outgoing, "sec", split_axis=0, concat_axis=0, tiled=True)
    my_sources = lax.dynamic_slice_in_dim(table, me_sec * sdev, sdev)
    sender = my_sources // sdev
    onehot = (sender[:, None] == jnp.arange(nsec, dtype=jnp.int32)[None, :]).astype(jnp.int32)
    slot_index = jnp.sum(jnp.cumsum(onehot, axis=0) * onehot, axis=1) - 1
    position = sender * slots + slot_index
    taken = jnp.take(arrived.reshape(nsec * slots, blk, phys, blk), position, axis=0)
    left = jnp.einsum(
        "wtab,tbpc->wtapc", left_env, taken, preferred_element_type=jnp.float32
    ).astype(jnp.bfloat16)
    mixed = jnp.einsum(
        "wtapc,wtpq->wtaqc", left, site_op, preferred_element_type=jnp.float32
    ).astype(jnp.bfloat16)
    partial_value = jnp.einsum(
        "wtaqc,wtcd->atqd", mixed, right_env, preferred_element_type=jnp.float32
    )
    summed = lax.psum_scatter(partial_value, "mpo", scatter_dimension=0, tiled=True)
    return summed.astype(jnp.bfloat16)


def shards(psi, left_env, right_env, site_op, source):
    nsec = lax.axis_size("sec")
    nmpo = lax.axis_size("mpo")
    exact = psi.shape[0] == SLOTS * nsec and nsec == 4 and nmpo == 4
    body = fast_shards if exact else any_shards
    return body(psi, left_env, right_env, site_op, source)


def solution(mesh):
    placed = (
        P(("grp", "sec"), None, None, None),
        P(("grp", "mpo"), "sec", None, None),
        P(("grp", "mpo"), "sec", None, None),
        P(("grp", "mpo"), "sec", None, None),
        P("mpo", None),
    )
    return jax.shard_map(
        shards,
        mesh=mesh,
        in_specs=placed,
        out_specs=P("mpo", ("grp", "sec"), None, None),
        check_vma=False,
    )
```

```python
import functools

import jax
import jax.numpy as jnp
from jax import lax
from jax.experimental import pallas as pl
from jax.experimental.pallas import tpu as pltpu
from jax.sharding import PartitionSpec as P

SLOTS = 2
EARLY = (0,)
MID = (2, 1)
LAST = 3
LATE = MID + (LAST,)
NAME_ROWS = 16
VMEM_BYTES = 16 * 1024 * 1024


def space(kind):
    return pl.BlockSpec(memory_space=kind)


def params():
    return pltpu.CompilerParams(vmem_limit_bytes=VMEM_BYTES)


def split(value, count):
    if count & (count - 1) == 0:
        shift = count.bit_length() - 1
        return jnp.right_shift(value, shift), jnp.bitwise_and(value, count - 1)
    owner = lax.div(value, jnp.int32(count))
    return owner, value - owner * count


def pick(table, base, count, block):
    zero = jnp.int32(0)
    seen, places, rows = zero, [zero, zero], [zero, zero]
    for t in range(count):
        owner, row = split(table[0, base + t], count)
        hit = owner == block
        for j in range(SLOTS):
            here = hit & (seen == j)
            places[j] = jnp.where(here, jnp.int32(t), places[j])
            rows[j] = jnp.where(here, row, rows[j])
        seen = seen + hit.astype(jnp.int32)
    return places, rows


def route_kernel(classes, source, psi, *refs):
    outs, (table, held, load, sems) = refs[: len(classes)], refs[len(classes) :]
    sdev = psi.shape[0]
    me = lax.axis_index("sec")
    fetch = pltpu.make_async_copy(source, table, load)
    fetch.start()
    copies = []
    for row in range(sdev):
        copy = pltpu.make_async_copy(psi.at[row], held.at[row], sems.at[row])
        copy.start()
        copies.append(copy)
    fetch.wait()
    rows = [pick(table, jnp.bitwise_xor(me, k) * sdev, sdev, me)[1] for k in classes]
    for copy in copies:
        copy.wait()
    for i in range(len(classes)):
        for j in range(SLOTS):
            outs[i][j] = held[rows[i][j]]


def route(classes, source, psi):
    block = psi.shape[1:]
    return pl.pallas_call(
        functools.partial(route_kernel, classes),
        out_shape=[jax.ShapeDtypeStruct((SLOTS,) + block, psi.dtype)] * len(classes),
        in_specs=[space(pl.ANY)] * 2,
        out_specs=[space(pltpu.VMEM)] * len(classes),
        scratch_shapes=[
            pltpu.SMEM(source.shape, jnp.int32),
            pltpu.VMEM(psi.shape, psi.dtype),
            pltpu.SemaphoreType.DMA,
            pltpu.SemaphoreType.DMA((psi.shape[0],)),
        ],
        compiler_params=params(),
        name="route",
    )(source, psi)


def double_kernel(block, out, sems):
    copies = [pltpu.make_async_copy(block, out.at[i], sems.at[i]) for i in range(2)]
    for copy in copies:
        copy.start()
    for copy in copies:
        copy.wait()


def double(block):
    return pl.pallas_call(
        double_kernel,
        out_shape=jax.ShapeDtypeStruct((2,) + block.shape, block.dtype),
        in_specs=[space(pltpu.VMEM)],
        out_specs=space(pl.ANY),
        scratch_shapes=[pltpu.SemaphoreType.DMA((2,))],
        compiler_params=params(),
        name="double",
    )(block)


def order_kernel(nsec, sdev, source, after, order, table, load):
    me = lax.axis_index("sec")
    fetch = pltpu.make_async_copy(source, table, load)
    fetch.start()
    fetch.wait()
    for k in range(nsec):
        places = pick(table, me * sdev, sdev, jnp.bitwise_xor(me, k))[0]
        for j in range(SLOTS):
            order[k * SLOTS + j] = places[j]


def receive_order(source, after, nsec, sdev):
    return pl.pallas_call(
        functools.partial(order_kernel, nsec, sdev),
        out_shape=jax.ShapeDtypeStruct((nsec * SLOTS,), jnp.int32),
        in_specs=[space(pl.ANY)] * 2,
        out_specs=space(pltpu.SMEM),
        scratch_shapes=[pltpu.SMEM(source.shape, jnp.int32), pltpu.SemaphoreType.DMA],
        compiler_params=params(),
        name="order",
    )(source, after)


def left_rows(lhs, block):
    wide = jnp.dot(lhs, jnp.concatenate(block, axis=1), preferred_element_type=jnp.float32)
    return wide.astype(jnp.bfloat16)


def right_rows(wide, rhs, op, wdev, phys):
    rows = wide.shape[0] // wdev
    blk = rhs.shape[1]
    outs = []
    for q in range(phys):
        across = []
        for w in range(wdev):
            total = None
            for p in range(phys):
                part = wide[w * rows : (w + 1) * rows, p * blk : (p + 1) * blk]
                term = part.astype(jnp.float32) * op(w, p, q)
                total = term if total is None else total + term
            across.append(total.astype(jnp.bfloat16))
        mixed = jnp.concatenate(across, axis=1)
        outs.append(jnp.dot(mixed, rhs, preferred_element_type=jnp.float32))
    return outs


def scalar_op(ops, t, sdev, phys):
    return lambda w, p, q: ops[(w * sdev + t) * (phys * phys) + p * phys + q]


def row_op(rows, s, phys):
    def op(w, p, q):
        i = (w * phys + p) * phys + q
        return rows[s, i : i + 1, :]

    return op


QUARTERS = (2, 0, 3, 1)


def early_kernel(nsec, nmpo, order, ops, *refs):
    blocks, refs = refs[: len(EARLY)], refs[len(EARLY) :]
    left, right, keep, far_give, near_give, lstage, rstage, oprows, named = refs
    wdev, sdev, blk = left.shape[:3]
    phys = blocks[0].shape[1]
    part = blk // nmpo
    me = lax.axis_index("mpo")

    def side(t):
        rows = []
        for w in range(wdev):
            for m in QUARTERS:
                start = pl.multiple_of(jnp.bitwise_xor(me, m) * part, part)
                rows.append(left[w, t, pl.ds(start, part), :])
        return jnp.concatenate(rows, axis=0)

    for s in range(len(LATE) * SLOTS):
        t = order[LATE[s // SLOTS] * SLOTS + s % SLOTS]
        lstage[s] = side(t)
        rstage[s] = right[:, t].reshape(wdev * blk, blk)
    line = lax.broadcasted_iota(jnp.int32, named.shape, 0)
    names = jnp.zeros(named.shape, jnp.float32)
    for s in range(SLOTS):
        t = order[LAST * SLOTS + s]
        names = jnp.where(line == s, t.astype(jnp.float32), names)
        op = scalar_op(ops, t, sdev, phys)
        for w in range(wdev):
            for p in range(phys):
                for q in range(phys):
                    i = (w * phys + p) * phys + q
                    oprows[s, i : i + 1, :] = jnp.full((1, blk), op(w, p, q), jnp.float32)
    named[...] = names.astype(named.dtype)
    for i, k in enumerate(EARLY):
        for j in range(SLOTS):
            s = i * SLOTS + j
            t = order[k * SLOTS + j]
            rhs = right[:, t].reshape(wdev * blk, blk)
            block = [blocks[i][j, p] for p in range(phys)]
            op = scalar_op(ops, t, sdev, phys)
            outs = right_rows(left_rows(side(t), block), rhs, op, wdev, phys)
            for q in range(phys):
                keep[0, s, q] = outs[q][:part]
                keep[1, s, q] = outs[q][part : 2 * part]
                far_give[s, q] = outs[q][2 * part : 3 * part].astype(jnp.bfloat16)
                near_give[s, q] = outs[q][3 * part :].astype(jnp.bfloat16)


def early(order, ops, blocks, left, right, nsec, nmpo):
    wdev, sdev, blk = left.shape[:3]
    phys = blocks[0].shape[1]
    part = blk // nmpo
    n, late_n = len(EARLY) * SLOTS, len(LATE) * SLOTS
    keep = jax.ShapeDtypeStruct((2, n, phys, part, blk), jnp.float32)
    give = jax.ShapeDtypeStruct((n, phys, part, blk), jnp.bfloat16)
    rows = jax.ShapeDtypeStruct((SLOTS, wdev * phys * phys, blk), jnp.float32)
    name = jax.ShapeDtypeStruct((NAME_ROWS, blk), jnp.bfloat16)
    whole = jax.ShapeDtypeStruct((late_n, wdev * blk, blk), jnp.bfloat16)
    return pl.pallas_call(
        functools.partial(early_kernel, nsec, nmpo),
        out_shape=[keep, give, give, whole, whole, rows, name],
        in_specs=[space(pltpu.SMEM)] * 2 + [space(pltpu.VMEM)] * (len(EARLY) + 2),
        out_specs=[space(pltpu.VMEM)] * 7,
        compiler_params=params(),
        cost_estimate=pl.CostEstimate(
            flops=n * wdev * phys * blk**3 * 4,
            bytes_accessed=8 * 1024 * 1024,
            transcendentals=0,
        ),
        name="early",
    )(order, ops, *blocks, left, right)


def mid_kernel(wdev, sdev, order_in, ops_in, *refs):
    nmid = len(MID)
    blocks, refs = refs[:nmid], refs[nmid:]
    lstage, rstage, early_keep, early_far, early_near, keep, far_give, near_give = refs[:8]
    order, ops, sems = refs[8:]
    phys, part = far_give.shape[1], far_give.shape[2]
    loads = [
        pltpu.make_async_copy(order_in, order, sems.at[0]),
        pltpu.make_async_copy(ops_in, ops, sems.at[1]),
    ]
    for load in loads:
        load.start()
    wides = []
    for s in range(nmid * SLOTS):
        block = [blocks[s // SLOTS][s % SLOTS, p] for p in range(phys)]
        wides.append(left_rows(lstage[s], block))
    for load in loads:
        load.wait()

    def place(classes, s):
        return order[classes[s // SLOTS] * SLOTS + s % SLOTS]

    for s in range(nmid * SLOTS):
        t = place(MID, s)
        outs = right_rows(wides[s], rstage[s], scalar_op(ops, t, sdev, phys), wdev, phys)
        for q in range(phys):
            keep[0, t, q] = outs[q][:part]
            keep[1, t, q] = outs[q][part : 2 * part]
            far_give[t, q] = outs[q][2 * part : 3 * part].astype(jnp.bfloat16)
            near_give[t, q] = outs[q][3 * part :].astype(jnp.bfloat16)
    for s in range(len(EARLY) * SLOTS):
        t = place(EARLY, s)
        for side in range(2):
            keep[side, t] = early_keep[side, s]
        far_give[t] = early_far[s]
        near_give[t] = early_near[s]
    for s in range(SLOTS):
        t = order[LAST * SLOTS + s]
        for side in range(2):
            keep[side, t] = jnp.zeros(keep.shape[2:], keep.dtype)
        far_give[t] = jnp.zeros(far_give.shape[1:], far_give.dtype)
        near_give[t] = jnp.zeros(near_give.shape[1:], near_give.dtype)


def mid(order, ops, blocks, staged, wdev, sdev):
    phys, part, blk = staged[0].shape[2:]
    n = len(blocks) * SLOTS
    give = jax.ShapeDtypeStruct((sdev, phys, part, blk), jnp.bfloat16)
    return pl.pallas_call(
        functools.partial(mid_kernel, wdev, sdev),
        out_shape=[jax.ShapeDtypeStruct((2, sdev, phys, part, blk), jnp.float32), give, give],
        in_specs=[space(pl.ANY)] * 2 + [space(pltpu.VMEM)] * (len(blocks) + 5),
        out_specs=[space(pltpu.VMEM)] * 3,
        scratch_shapes=[
            pltpu.SMEM(order.shape, order.dtype),
            pltpu.SMEM(ops.shape, ops.dtype),
            pltpu.SemaphoreType.DMA((2,)),
        ],
        compiler_params=params(),
        cost_estimate=pl.CostEstimate(
            flops=n * wdev * phys * blk**3 * 4,
            bytes_accessed=8 * 1024 * 1024,
            transcendentals=0,
        ),
        name="mid",
    )(order, ops, *blocks, *staged[3:5], *staged[:3])


def last_kernel(wdev, after, block, lstage, rstage, oprows, named, *gives):
    phys, blk = block.shape[2], block.shape[4]
    part = blk // len(gives)
    size = phys * part
    first = len(MID) * SLOTS
    me = lax.axis_index("sec")
    other = (jnp.bitwise_xor(me, LAST) > me).astype(jnp.int32)
    wides = []
    for s in range(SLOTS):
        wides.append(left_rows(lstage[first + s], [block[other, s, p] for p in range(phys)]))
    for s in range(SLOTS):
        outs = right_rows(wides[s], rstage[first + s], row_op(oprows, s, phys), wdev, phys)
        for i, m in enumerate(QUARTERS):
            for q in range(phys):
                rows = outs[q][i * part : (i + 1) * part].astype(gives[m].dtype)
                at = s * size + q * part
                gives[m][at : at + part] = rows
    for give in gives:
        give[SLOTS * size :] = named[...].astype(give.dtype)


def last(after, block, staged, wdev):
    phys, part, blk = staged[0].shape[2:]
    shape = (SLOTS * phys * part + NAME_ROWS, blk)
    give = jax.ShapeDtypeStruct(shape, jnp.bfloat16)
    return pl.pallas_call(
        functools.partial(last_kernel, wdev),
        out_shape=[jax.ShapeDtypeStruct(shape, jnp.float32)] + [give] * 3,
        in_specs=[space(pl.ANY)] + [space(pltpu.VMEM)] * 5,
        out_specs=[space(pltpu.VMEM)] * 4,
        compiler_params=params(),
        cost_estimate=pl.CostEstimate(
            flops=SLOTS * wdev * phys * blk**3 * 4,
            bytes_accessed=4 * 1024 * 1024,
            transcendentals=0,
        ),
        name="last",
    )(after, block, *staged[3:])


def pair_kernel(keep, got, out):
    out[...] = (keep[0] + got[...].astype(jnp.float32)).astype(out.dtype)


def pair(keep, got):
    return pl.pallas_call(
        pair_kernel,
        out_shape=jax.ShapeDtypeStruct(got.shape, got.dtype),
        in_specs=[space(pltpu.VMEM)] * 2,
        out_specs=space(pltpu.VMEM),
        compiler_params=params(),
        name="pair",
    )(keep, got)


def tail_sum(tails, t, first, count):
    total = None
    for tail in tails:
        end = tail.shape[0] - NAME_ROWS
        size = end // SLOTS
        names = tail[end:, :].astype(jnp.float32)
        for s in range(SLOTS):
            at = s * size + first
            rows = tail[at : at + count, :].astype(jnp.float32)
            value = jnp.where(names[s : s + 1] == t, rows, 0.0)
            total = value if total is None else total + value
    return total


def base_kernel(keep, near, far, own, mate, acc):
    sdev, phys, part, blk = acc.shape
    for t in range(sdev):
        total = keep[1, t] + near[t].astype(jnp.float32) + far[t].astype(jnp.float32)
        acc[t] = total + tail_sum((own, mate), t, 0, phys * part).reshape(phys, part, blk)


def base(keep, near, far, own, mate):
    return pl.pallas_call(
        base_kernel,
        out_shape=jax.ShapeDtypeStruct(far.shape, jnp.float32),
        in_specs=[space(pltpu.VMEM)] * 5,
        out_specs=space(pltpu.VMEM),
        compiler_params=params(),
        name="base",
    )(keep, near, far, own, mate)


def finish_kernel(total, tail2, tail3, out, acc, turned, sems):
    sdev, phys, part, blk = total.shape
    copies = []
    for q in range(phys):
        for t in range(sdev):
            acc[q, t] = total[t, q] + tail_sum((tail2, tail3), t, q * part, part)
        turned[q] = jnp.swapaxes(acc[q], 0, 1).astype(turned.dtype)
        copy = pltpu.make_async_copy(turned.at[q], out.at[:, q], sems.at[q])
        copy.start()
        copies.append(copy)
    for copy in copies:
        copy.wait()


def finish(total, tail2, tail3):
    sdev, phys, part, blk = total.shape
    return pl.pallas_call(
        finish_kernel,
        out_shape=jax.ShapeDtypeStruct((part, phys, sdev, blk), jnp.bfloat16),
        in_specs=[space(pltpu.VMEM)] * 3,
        out_specs=space(pl.ANY),
        scratch_shapes=[
            pltpu.VMEM((phys, sdev, part, blk), jnp.float32),
            pltpu.VMEM((phys, part, sdev, blk), jnp.bfloat16),
            pltpu.SemaphoreType.DMA((phys,)),
        ],
        compiler_params=params(),
        name="finish",
    )(total, tail2, tail3)


def fast_shards(psi, left_env, right_env, site_op, source):
    nsec = lax.axis_size("sec")
    nmpo = lax.axis_size("mpo")
    sdev = psi.shape[0]
    wdev = left_env.shape[0]
    blocks = jnp.transpose(psi, (0, 2, 1, 3))
    ops = site_op.astype(jnp.float32).reshape(-1)
    table = pltpu.with_memory_space_constraint(source, pltpu.HBM)
    pinned = pltpu.with_memory_space_constraint(blocks, pltpu.HBM)
    held = route(EARLY + MID + (LAST,), table, pinned)
    arrived = {0: held[0]}
    for k, value in zip(MID, held[len(EARLY) :]):
        arrived[k] = lax.ppermute(value, "sec", [(i, i ^ k) for i in range(nsec)])
    both = double(held[-1])
    order = receive_order(table, both, nsec, sdev)
    pairs = [[i, i ^ LAST] for i in range(nsec) if i < i ^ LAST]
    final = lax.all_to_all(both, "sec", 0, 0, axis_index_groups=pairs, tiled=True)

    def across(value, m):
        return lax.ppermute(value, "mpo", [(i, i ^ m) for i in range(nmpo)])

    staged = early(order, ops, [arrived[k] for k in EARLY], left_env, right_env, nsec, nmpo)
    keep, far_give, near_give = mid(order, ops, [arrived[k] for k in MID], staged, wdev, sdev)
    summed = pair(keep, across(far_give, 1))
    far = across(summed, 2)
    near = across(near_give, 1)
    own, give1, give2, give3 = last(summed, final, staged, wdev)
    total = base(keep, near, far, own, across(give1, 1))
    out = finish(total, across(give2, 2), across(give3, 3))
    return jnp.transpose(out, (0, 2, 1, 3))


def any_shards(psi, left_env, right_env, site_op, source):
    me_sec = lax.axis_index("sec")
    nsec = lax.axis_size("sec")
    sdev = psi.shape[0]
    blk = psi.shape[1]
    phys = psi.shape[2]
    slots = max(2, (sdev + nsec - 1) // nsec)
    table = source[0]
    owners = (table // sdev).reshape(nsec, sdev)
    mine = owners == me_sec
    ranked = jnp.cumsum(mine.astype(jnp.int32), axis=1) - 1
    picked = mine[:, None, :] & (
        ranked[:, None, :] == jnp.arange(slots, dtype=jnp.int32)[None, :, None]
    )
    local_rows = (table % sdev).reshape(nsec, sdev)
    chosen = jnp.sum(jnp.where(picked, local_rows[:, None, :], 0), axis=2)
    outgoing = jnp.take(psi, chosen.reshape(-1), axis=0).reshape(nsec, slots, blk, phys, blk)
    arrived = lax.all_to_all(outgoing, "sec", split_axis=0, concat_axis=0, tiled=True)
    my_sources = lax.dynamic_slice_in_dim(table, me_sec * sdev, sdev)
    sender = my_sources // sdev
    onehot = (sender[:, None] == jnp.arange(nsec, dtype=jnp.int32)[None, :]).astype(jnp.int32)
    slot_index = jnp.sum(jnp.cumsum(onehot, axis=0) * onehot, axis=1) - 1
    position = sender * slots + slot_index
    taken = jnp.take(arrived.reshape(nsec * slots, blk, phys, blk), position, axis=0)
    left = jnp.einsum(
        "wtab,tbpc->wtapc", left_env, taken, preferred_element_type=jnp.float32
    ).astype(jnp.bfloat16)
    mixed = jnp.einsum(
        "wtapc,wtpq->wtaqc", left, site_op, preferred_element_type=jnp.float32
    ).astype(jnp.bfloat16)
    partial_value = jnp.einsum(
        "wtaqc,wtcd->atqd", mixed, right_env, preferred_element_type=jnp.float32
    )
    summed = lax.psum_scatter(partial_value, "mpo", scatter_dimension=0, tiled=True)
    return summed.astype(jnp.bfloat16)


def shards(psi, left_env, right_env, site_op, source):
    nsec = lax.axis_size("sec")
    nmpo = lax.axis_size("mpo")
    exact = psi.shape[0] == SLOTS * nsec and nsec == 4 and nmpo == 4
    body = fast_shards if exact else any_shards
    return body(psi, left_env, right_env, site_op, source)


def solution(mesh):
    placed = (
        P(("grp", "sec"), None, None, None),
        P(("grp", "mpo"), "sec", None, None),
        P(("grp", "mpo"), "sec", None, None),
        P(("grp", "mpo"), "sec", None, None),
        P("mpo", None),
    )
    return jax.shard_map(
        shards,
        mesh=mesh,
        in_specs=placed,
        out_specs=P("mpo", ("grp", "sec"), None, None),
        check_vma=False,
    )
```

```python
import functools

import jax
import jax.numpy as jnp
from jax import lax
from jax.experimental import pallas as pl
from jax.experimental.pallas import tpu as pltpu
from jax.sharding import PartitionSpec as P

SLOTS = 2
EARLY = (0,)
MID = (2, 1)
LAST = 3
LATE = MID + (LAST,)
NAME_ROWS = 16
VMEM_BYTES = 16 * 1024 * 1024


def space(kind):
    return pl.BlockSpec(memory_space=kind)


def params():
    return pltpu.CompilerParams(vmem_limit_bytes=VMEM_BYTES)


def split(value, count):
    if count & (count - 1) == 0:
        shift = count.bit_length() - 1
        return jnp.right_shift(value, shift), jnp.bitwise_and(value, count - 1)
    owner = lax.div(value, jnp.int32(count))
    return owner, value - owner * count


def pick(table, base, count, block):
    zero = jnp.int32(0)
    seen, places, rows = zero, [zero, zero], [zero, zero]
    for t in range(count):
        owner, row = split(table[0, base + t], count)
        hit = owner == block
        for j in range(SLOTS):
            here = hit & (seen == j)
            places[j] = jnp.where(here, jnp.int32(t), places[j])
            rows[j] = jnp.where(here, row, rows[j])
        seen = seen + hit.astype(jnp.int32)
    return places, rows


def route_kernel(classes, source, psi, *refs):
    outs, (table, held, load, sems) = refs[: len(classes)], refs[len(classes) :]
    sdev = psi.shape[0]
    me = lax.axis_index("sec")
    fetch = pltpu.make_async_copy(source, table, load)
    fetch.start()
    copies = []
    copy = pltpu.make_async_copy(psi, held, sems.at[0])
    copy.start()
    copies.append(copy)
    fetch.wait()
    rows = [pick(table, jnp.bitwise_xor(me, k) * sdev, sdev, me)[1] for k in classes]
    for copy in copies:
        copy.wait()
    for i in range(len(classes)):
        for j in range(SLOTS):
            outs[i][j] = held[rows[i][j]]


def route(classes, source, psi):
    block = psi.shape[1:]
    return pl.pallas_call(
        functools.partial(route_kernel, classes),
        out_shape=[jax.ShapeDtypeStruct((SLOTS,) + block, psi.dtype)] * len(classes),
        in_specs=[space(pl.ANY)] * 2,
        out_specs=[space(pltpu.VMEM)] * len(classes),
        scratch_shapes=[
            pltpu.SMEM(source.shape, jnp.int32),
            pltpu.VMEM(psi.shape, psi.dtype),
            pltpu.SemaphoreType.DMA,
            pltpu.SemaphoreType.DMA((1,)),
        ],
        compiler_params=params(),
        name="route",
    )(source, psi)


def double_kernel(block, out, sems):
    copies = [pltpu.make_async_copy(block, out.at[i], sems.at[i]) for i in range(2)]
    for copy in copies:
        copy.start()
    for copy in copies:
        copy.wait()


def double(block):
    return pl.pallas_call(
        double_kernel,
        out_shape=jax.ShapeDtypeStruct((2,) + block.shape, block.dtype),
        in_specs=[space(pltpu.VMEM)],
        out_specs=space(pl.ANY),
        scratch_shapes=[pltpu.SemaphoreType.DMA((2,))],
        compiler_params=params(),
        name="double",
    )(block)


def order_kernel(nsec, sdev, source, after, order, table, load):
    me = lax.axis_index("sec")
    fetch = pltpu.make_async_copy(source, table, load)
    fetch.start()
    fetch.wait()
    for k in range(nsec):
        places = pick(table, me * sdev, sdev, jnp.bitwise_xor(me, k))[0]
        for j in range(SLOTS):
            order[k * SLOTS + j] = places[j]


def receive_order(source, after, nsec, sdev):
    return pl.pallas_call(
        functools.partial(order_kernel, nsec, sdev),
        out_shape=jax.ShapeDtypeStruct((nsec * SLOTS,), jnp.int32),
        in_specs=[space(pl.ANY)] * 2,
        out_specs=space(pltpu.SMEM),
        scratch_shapes=[pltpu.SMEM(source.shape, jnp.int32), pltpu.SemaphoreType.DMA],
        compiler_params=params(),
        name="order",
    )(source, after)


def left_rows(lhs, block):
    wide = jnp.dot(lhs, jnp.concatenate(block, axis=1), preferred_element_type=jnp.float32)
    return wide.astype(jnp.bfloat16)


def right_rows(wide, rhs, op, wdev, phys):
    rows = wide.shape[0] // wdev
    blk = rhs.shape[1]
    outs = []
    for q in range(phys):
        across = []
        for w in range(wdev):
            total = None
            for p in range(phys):
                part = wide[w * rows : (w + 1) * rows, p * blk : (p + 1) * blk]
                term = part.astype(jnp.float32) * op(w, p, q)
                total = term if total is None else total + term
            across.append(total.astype(jnp.bfloat16))
        mixed = jnp.concatenate(across, axis=1)
        outs.append(jnp.dot(mixed, rhs, preferred_element_type=jnp.float32))
    return outs


def scalar_op(ops, t, sdev, phys):
    return lambda w, p, q: ops[(w * sdev + t) * (phys * phys) + p * phys + q]


def row_op(rows, s, phys):
    def op(w, p, q):
        i = (w * phys + p) * phys + q
        return rows[s, i : i + 1, :]

    return op


QUARTERS = (2, 0, 3, 1)


def early_kernel(nsec, nmpo, order, ops, *refs):
    blocks, refs = refs[: len(EARLY)], refs[len(EARLY) :]
    left, right, keep, far_give, near_give, lstage, rstage, oprows, named = refs
    wdev, sdev, blk = left.shape[:3]
    phys = blocks[0].shape[1]
    part = blk // nmpo
    me = lax.axis_index("mpo")

    def side(t):
        rows = []
        for w in range(wdev):
            for m in QUARTERS:
                start = pl.multiple_of(jnp.bitwise_xor(me, m) * part, part)
                rows.append(left[w, t, pl.ds(start, part), :])
        return jnp.concatenate(rows, axis=0)

    for s in range(len(LATE) * SLOTS):
        t = order[LATE[s // SLOTS] * SLOTS + s % SLOTS]
        lstage[s] = side(t)
        rstage[s] = right[:, t].reshape(wdev * blk, blk)
    line = lax.broadcasted_iota(jnp.int32, named.shape, 0)
    names = jnp.zeros(named.shape, jnp.float32)
    for s in range(SLOTS):
        t = order[LAST * SLOTS + s]
        names = jnp.where(line == s, t.astype(jnp.float32), names)
        op = scalar_op(ops, t, sdev, phys)
        for w in range(wdev):
            for p in range(phys):
                for q in range(phys):
                    i = (w * phys + p) * phys + q
                    oprows[s, i : i + 1, :] = jnp.full((1, blk), op(w, p, q), jnp.float32)
    named[...] = names.astype(named.dtype)
    for i, k in enumerate(EARLY):
        for j in range(SLOTS):
            s = i * SLOTS + j
            t = order[k * SLOTS + j]
            rhs = right[:, t].reshape(wdev * blk, blk)
            block = [blocks[i][j, p] for p in range(phys)]
            op = scalar_op(ops, t, sdev, phys)
            outs = right_rows(left_rows(side(t), block), rhs, op, wdev, phys)
            for q in range(phys):
                keep[0, s, q] = outs[q][:part]
                keep[1, s, q] = outs[q][part : 2 * part]
                far_give[s, q] = outs[q][2 * part : 3 * part].astype(jnp.bfloat16)
                near_give[s, q] = outs[q][3 * part :].astype(jnp.bfloat16)


def early(order, ops, blocks, left, right, nsec, nmpo):
    wdev, sdev, blk = left.shape[:3]
    phys = blocks[0].shape[1]
    part = blk // nmpo
    n, late_n = len(EARLY) * SLOTS, len(LATE) * SLOTS
    keep = jax.ShapeDtypeStruct((2, n, phys, part, blk), jnp.float32)
    give = jax.ShapeDtypeStruct((n, phys, part, blk), jnp.bfloat16)
    rows = jax.ShapeDtypeStruct((SLOTS, wdev * phys * phys, blk), jnp.float32)
    name = jax.ShapeDtypeStruct((NAME_ROWS, blk), jnp.bfloat16)
    whole = jax.ShapeDtypeStruct((late_n, wdev * blk, blk), jnp.bfloat16)
    return pl.pallas_call(
        functools.partial(early_kernel, nsec, nmpo),
        out_shape=[keep, give, give, whole, whole, rows, name],
        in_specs=[space(pltpu.SMEM)] * 2 + [space(pltpu.VMEM)] * (len(EARLY) + 2),
        out_specs=[space(pltpu.VMEM)] * 7,
        compiler_params=params(),
        cost_estimate=pl.CostEstimate(
            flops=n * wdev * phys * blk**3 * 4,
            bytes_accessed=8 * 1024 * 1024,
            transcendentals=0,
        ),
        name="early",
    )(order, ops, *blocks, left, right)


def mid_kernel(wdev, sdev, order_in, ops_in, *refs):
    nmid = len(MID)
    blocks, refs = refs[:nmid], refs[nmid:]
    lstage, rstage, early_keep, early_far, early_near, keep, far_give, near_give = refs[:8]
    order, ops, sems = refs[8:]
    phys, part = far_give.shape[1], far_give.shape[2]
    loads = [
        pltpu.make_async_copy(order_in, order, sems.at[0]),
        pltpu.make_async_copy(ops_in, ops, sems.at[1]),
    ]
    for load in loads:
        load.start()
    wides = []
    for s in range(nmid * SLOTS):
        block = [blocks[s // SLOTS][s % SLOTS, p] for p in range(phys)]
        wides.append(left_rows(lstage[s], block))
    for load in loads:
        load.wait()

    def place(classes, s):
        return order[classes[s // SLOTS] * SLOTS + s % SLOTS]

    for s in range(nmid * SLOTS):
        t = place(MID, s)
        outs = right_rows(wides[s], rstage[s], scalar_op(ops, t, sdev, phys), wdev, phys)
        for q in range(phys):
            keep[0, t, q] = outs[q][:part]
            keep[1, t, q] = outs[q][part : 2 * part]
            far_give[t, q] = outs[q][2 * part : 3 * part].astype(jnp.bfloat16)
            near_give[t, q] = outs[q][3 * part :].astype(jnp.bfloat16)
    for s in range(len(EARLY) * SLOTS):
        t = place(EARLY, s)
        for side in range(2):
            keep[side, t] = early_keep[side, s]
        far_give[t] = early_far[s]
        near_give[t] = early_near[s]
    for s in range(SLOTS):
        t = order[LAST * SLOTS + s]
        for side in range(2):
            keep[side, t] = jnp.zeros(keep.shape[2:], keep.dtype)
        far_give[t] = jnp.zeros(far_give.shape[1:], far_give.dtype)
        near_give[t] = jnp.zeros(near_give.shape[1:], near_give.dtype)


def mid(order, ops, blocks, staged, wdev, sdev):
    phys, part, blk = staged[0].shape[2:]
    n = len(blocks) * SLOTS
    give = jax.ShapeDtypeStruct((sdev, phys, part, blk), jnp.bfloat16)
    return pl.pallas_call(
        functools.partial(mid_kernel, wdev, sdev),
        out_shape=[jax.ShapeDtypeStruct((2, sdev, phys, part, blk), jnp.float32), give, give],
        in_specs=[space(pl.ANY)] * 2 + [space(pltpu.VMEM)] * (len(blocks) + 5),
        out_specs=[space(pltpu.VMEM)] * 3,
        scratch_shapes=[
            pltpu.SMEM(order.shape, order.dtype),
            pltpu.SMEM(ops.shape, ops.dtype),
            pltpu.SemaphoreType.DMA((2,)),
        ],
        compiler_params=params(),
        cost_estimate=pl.CostEstimate(
            flops=n * wdev * phys * blk**3 * 4,
            bytes_accessed=8 * 1024 * 1024,
            transcendentals=0,
        ),
        name="mid",
    )(order, ops, *blocks, *staged[3:5], *staged[:3])


def last_kernel(wdev, after, block, lstage, rstage, oprows, named, *gives):
    phys, blk = block.shape[2], block.shape[4]
    part = blk // len(gives)
    size = phys * part
    first = len(MID) * SLOTS
    me = lax.axis_index("sec")
    other = (jnp.bitwise_xor(me, LAST) > me).astype(jnp.int32)
    wides = []
    for s in range(SLOTS):
        wides.append(left_rows(lstage[first + s], [block[other, s, p] for p in range(phys)]))
    for s in range(SLOTS):
        outs = right_rows(wides[s], rstage[first + s], row_op(oprows, s, phys), wdev, phys)
        for i, m in enumerate(QUARTERS):
            for q in range(phys):
                rows = outs[q][i * part : (i + 1) * part].astype(gives[m].dtype)
                at = s * size + q * part
                gives[m][at : at + part] = rows
    for give in gives:
        give[SLOTS * size :] = named[...].astype(give.dtype)


def last(after, block, staged, wdev):
    phys, part, blk = staged[0].shape[2:]
    shape = (SLOTS * phys * part + NAME_ROWS, blk)
    give = jax.ShapeDtypeStruct(shape, jnp.bfloat16)
    return pl.pallas_call(
        functools.partial(last_kernel, wdev),
        out_shape=[jax.ShapeDtypeStruct(shape, jnp.float32)] + [give] * 3,
        in_specs=[space(pl.ANY)] + [space(pltpu.VMEM)] * 5,
        out_specs=[space(pltpu.VMEM)] * 4,
        compiler_params=params(),
        cost_estimate=pl.CostEstimate(
            flops=SLOTS * wdev * phys * blk**3 * 4,
            bytes_accessed=4 * 1024 * 1024,
            transcendentals=0,
        ),
        name="last",
    )(after, block, *staged[3:])


def pair_kernel(keep, got, out):
    out[...] = (keep[0] + got[...].astype(jnp.float32)).astype(out.dtype)


def pair(keep, got):
    return pl.pallas_call(
        pair_kernel,
        out_shape=jax.ShapeDtypeStruct(got.shape, got.dtype),
        in_specs=[space(pltpu.VMEM)] * 2,
        out_specs=space(pltpu.VMEM),
        compiler_params=params(),
        name="pair",
    )(keep, got)


def tail_sum(tails, t, first, count):
    total = None
    for tail in tails:
        end = tail.shape[0] - NAME_ROWS
        size = end // SLOTS
        names = tail[end:, :].astype(jnp.float32)
        for s in range(SLOTS):
            at = s * size + first
            rows = tail[at : at + count, :].astype(jnp.float32)
            value = jnp.where(names[s : s + 1] == t, rows, 0.0)
            total = value if total is None else total + value
    return total


def base_kernel(keep, near, far, own, mate, acc):
    sdev, phys, part, blk = acc.shape
    for t in range(sdev):
        total = keep[1, t] + near[t].astype(jnp.float32) + far[t].astype(jnp.float32)
        acc[t] = total + tail_sum((own, mate), t, 0, phys * part).reshape(phys, part, blk)


def base(keep, near, far, own, mate):
    return pl.pallas_call(
        base_kernel,
        out_shape=jax.ShapeDtypeStruct(far.shape, jnp.float32),
        in_specs=[space(pltpu.VMEM)] * 5,
        out_specs=space(pltpu.VMEM),
        compiler_params=params(),
        name="base",
    )(keep, near, far, own, mate)


def finish_kernel(total, tail2, tail3, out, acc, turned, sems):
    sdev, phys, part, blk = total.shape
    copies = []
    for q in range(phys):
        for t in range(sdev):
            acc[q, t] = total[t, q] + tail_sum((tail2, tail3), t, q * part, part)
        turned[q] = jnp.swapaxes(acc[q], 0, 1).astype(turned.dtype)
        copy = pltpu.make_async_copy(turned.at[q], out.at[:, q], sems.at[q])
        copy.start()
        copies.append(copy)
    for copy in copies:
        copy.wait()


def finish(total, tail2, tail3):
    sdev, phys, part, blk = total.shape
    return pl.pallas_call(
        finish_kernel,
        out_shape=jax.ShapeDtypeStruct((part, phys, sdev, blk), jnp.bfloat16),
        in_specs=[space(pltpu.VMEM)] * 3,
        out_specs=space(pl.ANY),
        scratch_shapes=[
            pltpu.VMEM((phys, sdev, part, blk), jnp.float32),
            pltpu.VMEM((phys, part, sdev, blk), jnp.bfloat16),
            pltpu.SemaphoreType.DMA((phys,)),
        ],
        compiler_params=params(),
        name="finish",
    )(total, tail2, tail3)


def fast_shards(psi, left_env, right_env, site_op, source):
    nsec = lax.axis_size("sec")
    nmpo = lax.axis_size("mpo")
    sdev = psi.shape[0]
    wdev = left_env.shape[0]
    blocks = jnp.transpose(psi, (0, 2, 1, 3))
    ops = site_op.astype(jnp.float32).reshape(-1)
    table = pltpu.with_memory_space_constraint(source, pltpu.HBM)
    pinned = pltpu.with_memory_space_constraint(blocks, pltpu.HBM)
    held = route(EARLY + MID + (LAST,), table, pinned)
    arrived = {0: held[0]}
    for k, value in zip(MID, held[len(EARLY) :]):
        arrived[k] = lax.ppermute(value, "sec", [(i, i ^ k) for i in range(nsec)])
    both = double(held[-1])
    order = receive_order(table, both, nsec, sdev)
    pairs = [[i, i ^ LAST] for i in range(nsec) if i < i ^ LAST]
    final = lax.all_to_all(both, "sec", 0, 0, axis_index_groups=pairs, tiled=True)

    def across(value, m):
        return lax.ppermute(value, "mpo", [(i, i ^ m) for i in range(nmpo)])

    staged = early(order, ops, [arrived[k] for k in EARLY], left_env, right_env, nsec, nmpo)
    keep, far_give, near_give = mid(order, ops, [arrived[k] for k in MID], staged, wdev, sdev)
    summed = pair(keep, across(far_give, 1))
    far = across(summed, 2)
    near = across(near_give, 1)
    own, give1, give2, give3 = last(summed, final, staged, wdev)
    total = base(keep, near, far, own, across(give1, 1))
    out = finish(total, across(give2, 2), across(give3, 3))
    return jnp.transpose(out, (0, 2, 1, 3))


def any_shards(psi, left_env, right_env, site_op, source):
    me_sec = lax.axis_index("sec")
    nsec = lax.axis_size("sec")
    sdev = psi.shape[0]
    blk = psi.shape[1]
    phys = psi.shape[2]
    slots = max(2, (sdev + nsec - 1) // nsec)
    table = source[0]
    owners = (table // sdev).reshape(nsec, sdev)
    mine = owners == me_sec
    ranked = jnp.cumsum(mine.astype(jnp.int32), axis=1) - 1
    picked = mine[:, None, :] & (
        ranked[:, None, :] == jnp.arange(slots, dtype=jnp.int32)[None, :, None]
    )
    local_rows = (table % sdev).reshape(nsec, sdev)
    chosen = jnp.sum(jnp.where(picked, local_rows[:, None, :], 0), axis=2)
    outgoing = jnp.take(psi, chosen.reshape(-1), axis=0).reshape(nsec, slots, blk, phys, blk)
    arrived = lax.all_to_all(outgoing, "sec", split_axis=0, concat_axis=0, tiled=True)
    my_sources = lax.dynamic_slice_in_dim(table, me_sec * sdev, sdev)
    sender = my_sources // sdev
    onehot = (sender[:, None] == jnp.arange(nsec, dtype=jnp.int32)[None, :]).astype(jnp.int32)
    slot_index = jnp.sum(jnp.cumsum(onehot, axis=0) * onehot, axis=1) - 1
    position = sender * slots + slot_index
    taken = jnp.take(arrived.reshape(nsec * slots, blk, phys, blk), position, axis=0)
    left = jnp.einsum(
        "wtab,tbpc->wtapc", left_env, taken, preferred_element_type=jnp.float32
    ).astype(jnp.bfloat16)
    mixed = jnp.einsum(
        "wtapc,wtpq->wtaqc", left, site_op, preferred_element_type=jnp.float32
    ).astype(jnp.bfloat16)
    partial_value = jnp.einsum(
        "wtaqc,wtcd->atqd", mixed, right_env, preferred_element_type=jnp.float32
    )
    summed = lax.psum_scatter(partial_value, "mpo", scatter_dimension=0, tiled=True)
    return summed.astype(jnp.bfloat16)


def shards(psi, left_env, right_env, site_op, source):
    nsec = lax.axis_size("sec")
    nmpo = lax.axis_size("mpo")
    exact = psi.shape[0] == SLOTS * nsec and nsec == 4 and nmpo == 4
    body = fast_shards if exact else any_shards
    return body(psi, left_env, right_env, site_op, source)


def solution(mesh):
    placed = (
        P(("grp", "sec"), None, None, None),
        P(("grp", "mpo"), "sec", None, None),
        P(("grp", "mpo"), "sec", None, None),
        P(("grp", "mpo"), "sec", None, None),
        P("mpo", None),
    )
    return jax.shard_map(
        shards,
        mesh=mesh,
        in_specs=placed,
        out_specs=P("mpo", ("grp", "sec"), None, None),
        check_vma=False,
    )
```

```python
import functools

import jax
import jax.numpy as jnp
from jax import lax
from jax.experimental import pallas as pl
from jax.experimental.pallas import tpu as pltpu
from jax.sharding import PartitionSpec as P

SLOTS = 2
EARLY = (0,)
MID = (2, 1)
LAST = 3
LATE = MID + (LAST,)
NAME_ROWS = 16
VMEM_BYTES = 16 * 1024 * 1024


def space(kind):
    return pl.BlockSpec(memory_space=kind)


def params():
    return pltpu.CompilerParams(vmem_limit_bytes=VMEM_BYTES)


def split(value, count):
    if count & (count - 1) == 0:
        shift = count.bit_length() - 1
        return jnp.right_shift(value, shift), jnp.bitwise_and(value, count - 1)
    owner = lax.div(value, jnp.int32(count))
    return owner, value - owner * count


def pick(table, base, count, block):
    zero = jnp.int32(0)
    seen, places, rows = zero, [zero, zero], [zero, zero]
    for t in range(count):
        owner, row = split(table[0, base + t], count)
        hit = owner == block
        for j in range(SLOTS):
            here = hit & (seen == j)
            places[j] = jnp.where(here, jnp.int32(t), places[j])
            rows[j] = jnp.where(here, row, rows[j])
        seen = seen + hit.astype(jnp.int32)
    return places, rows


def route_kernel(classes, source, psi, *refs):
    outs, (table, held, load, sems) = refs[: len(classes)], refs[len(classes) :]
    sdev = psi.shape[0]
    me = lax.axis_index("sec")
    fetch = pltpu.make_async_copy(source, table, load)
    fetch.start()
    copies = []
    copy = pltpu.make_async_copy(psi, held, sems.at[0])
    copy.start()
    copies.append(copy)
    fetch.wait()
    rows = [pick(table, jnp.bitwise_xor(me, k) * sdev, sdev, me)[1] for k in classes]
    for copy in copies:
        copy.wait()
    for i in range(len(classes)):
        for j in range(SLOTS):
            outs[i][j] = held[rows[i][j]]


def route(classes, source, psi):
    block = psi.shape[1:]
    return pl.pallas_call(
        functools.partial(route_kernel, classes),
        out_shape=[jax.ShapeDtypeStruct((SLOTS,) + block, psi.dtype)] * len(classes),
        in_specs=[space(pl.ANY)] * 2,
        out_specs=[space(pltpu.VMEM)] * len(classes),
        scratch_shapes=[
            pltpu.SMEM(source.shape, jnp.int32),
            pltpu.VMEM(psi.shape, psi.dtype),
            pltpu.SemaphoreType.DMA,
            pltpu.SemaphoreType.DMA((1,)),
        ],
        compiler_params=params(),
        name="route",
    )(source, psi)


def double_kernel(block, out, sems):
    copies = [pltpu.make_async_copy(block, out.at[i], sems.at[i]) for i in range(2)]
    for copy in copies:
        copy.start()
    for copy in copies:
        copy.wait()


def double(block):
    return pl.pallas_call(
        double_kernel,
        out_shape=jax.ShapeDtypeStruct((2,) + block.shape, block.dtype),
        in_specs=[space(pltpu.VMEM)],
        out_specs=space(pl.ANY),
        scratch_shapes=[pltpu.SemaphoreType.DMA((2,))],
        compiler_params=params(),
        name="double",
    )(block)


def order_kernel(nsec, sdev, source, after, order, table, load):
    me = lax.axis_index("sec")
    fetch = pltpu.make_async_copy(source, table, load)
    fetch.start()
    fetch.wait()
    for k in range(nsec):
        places = pick(table, me * sdev, sdev, jnp.bitwise_xor(me, k))[0]
        for j in range(SLOTS):
            order[k * SLOTS + j] = places[j]


def receive_order(source, after, nsec, sdev):
    return pl.pallas_call(
        functools.partial(order_kernel, nsec, sdev),
        out_shape=jax.ShapeDtypeStruct((nsec * SLOTS,), jnp.int32),
        in_specs=[space(pl.ANY)] * 2,
        out_specs=space(pltpu.SMEM),
        scratch_shapes=[pltpu.SMEM(source.shape, jnp.int32), pltpu.SemaphoreType.DMA],
        compiler_params=params(),
        name="order",
    )(source, after)


def left_rows(lhs, block):
    wide = jnp.dot(lhs, jnp.concatenate(block, axis=1), preferred_element_type=jnp.float32)
    return wide.astype(jnp.bfloat16)


def right_rows(wide, rhs, op, wdev, phys):
    rows = wide.shape[0] // wdev
    blk = rhs.shape[1]
    outs = []
    for q in range(phys):
        across = []
        for w in range(wdev):
            total = None
            for p in range(phys):
                part = wide[w * rows : (w + 1) * rows, p * blk : (p + 1) * blk]
                term = part.astype(jnp.float32) * op(w, p, q)
                total = term if total is None else total + term
            across.append(total.astype(jnp.bfloat16))
        mixed = jnp.concatenate(across, axis=1)
        outs.append(jnp.dot(mixed, rhs, preferred_element_type=jnp.float32))
    return outs


def scalar_op(ops, t, sdev, phys):
    return lambda w, p, q: ops[(w * sdev + t) * (phys * phys) + p * phys + q]


def row_op(rows, s, phys):
    def op(w, p, q):
        i = (w * phys + p) * phys + q
        return rows[s, i : i + 1, :]

    return op


QUARTERS = (2, 0, 3, 1)


def early_kernel(nsec, nmpo, order, ops, *refs):
    blocks, refs = refs[: len(EARLY)], refs[len(EARLY) :]
    left, right, keep, far_give, near_give, lstage, rstage, oprows, named = refs
    wdev, sdev, blk = left.shape[:3]
    phys = blocks[0].shape[1]
    part = blk // nmpo
    me = lax.axis_index("mpo")

    def side(t):
        rows = []
        for w in range(wdev):
            for m in QUARTERS:
                start = pl.multiple_of(jnp.bitwise_xor(me, m) * part, part)
                rows.append(left[w, t, pl.ds(start, part), :])
        return jnp.concatenate(rows, axis=0)

    for s in range(len(LATE) * SLOTS):
        t = order[LATE[s // SLOTS] * SLOTS + s % SLOTS]
        lstage[s] = side(t)
        rstage[s] = right[:, t].reshape(wdev * blk, blk)
    line = lax.broadcasted_iota(jnp.int32, named.shape, 0)
    names = jnp.zeros(named.shape, jnp.float32)
    for s in range(SLOTS):
        t = order[LAST * SLOTS + s]
        names = jnp.where(line == s, t.astype(jnp.float32), names)
        op = scalar_op(ops, t, sdev, phys)
        for w in range(wdev):
            for p in range(phys):
                for q in range(phys):
                    i = (w * phys + p) * phys + q
                    oprows[s, i : i + 1, :] = jnp.full((1, blk), op(w, p, q), jnp.float32)
    named[...] = names.astype(named.dtype)
    for i, k in enumerate(EARLY):
        for j in range(SLOTS):
            s = i * SLOTS + j
            t = order[k * SLOTS + j]
            rhs = right[:, t].reshape(wdev * blk, blk)
            block = [blocks[i][j, p] for p in range(phys)]
            op = scalar_op(ops, t, sdev, phys)
            outs = right_rows(left_rows(side(t), block), rhs, op, wdev, phys)
            for q in range(phys):
                keep[0, s, q] = outs[q][:part]
                keep[1, s, q] = outs[q][part : 2 * part]
                far_give[s, q] = outs[q][2 * part : 3 * part].astype(jnp.bfloat16)
                near_give[s, q] = outs[q][3 * part :].astype(jnp.bfloat16)


def early(order, ops, blocks, left, right, nsec, nmpo):
    wdev, sdev, blk = left.shape[:3]
    phys = blocks[0].shape[1]
    part = blk // nmpo
    n, late_n = len(EARLY) * SLOTS, len(LATE) * SLOTS
    keep = jax.ShapeDtypeStruct((2, n, phys, part, blk), jnp.float32)
    give = jax.ShapeDtypeStruct((n, phys, part, blk), jnp.bfloat16)
    rows = jax.ShapeDtypeStruct((SLOTS, wdev * phys * phys, blk), jnp.float32)
    name = jax.ShapeDtypeStruct((NAME_ROWS, blk), jnp.bfloat16)
    whole = jax.ShapeDtypeStruct((late_n, wdev * blk, blk), jnp.bfloat16)
    return pl.pallas_call(
        functools.partial(early_kernel, nsec, nmpo),
        out_shape=[keep, give, give, whole, whole, rows, name],
        in_specs=[space(pltpu.SMEM)] * 2 + [space(pltpu.VMEM)] * (len(EARLY) + 2),
        out_specs=[space(pltpu.VMEM)] * 7,
        compiler_params=params(),
        cost_estimate=pl.CostEstimate(
            flops=n * wdev * phys * blk**3 * 4,
            bytes_accessed=8 * 1024 * 1024,
            transcendentals=0,
        ),
        name="early",
    )(order, ops, *blocks, left, right)


def mid_kernel(wdev, sdev, order_in, ops_in, *refs):
    nmid = len(MID)
    blocks, refs = refs[:nmid], refs[nmid:]
    lstage, rstage, early_keep, early_far, early_near, keep, far_give, near_give = refs[:8]
    order, ops, sems = refs[8:]
    phys, part = far_give.shape[1], far_give.shape[2]
    loads = [
        pltpu.make_async_copy(order_in, order, sems.at[0]),
        pltpu.make_async_copy(ops_in, ops, sems.at[1]),
    ]
    for load in loads:
        load.start()
    wides = []
    for s in range(nmid * SLOTS):
        block = [blocks[s // SLOTS][s % SLOTS, p] for p in range(phys)]
        wides.append(left_rows(lstage[s], block))
    for load in loads:
        load.wait()

    def place(classes, s):
        return order[classes[s // SLOTS] * SLOTS + s % SLOTS]

    for s in range(nmid * SLOTS):
        t = place(MID, s)
        outs = right_rows(wides[s], rstage[s], scalar_op(ops, t, sdev, phys), wdev, phys)
        for q in range(phys):
            keep[0, t, q] = outs[q][:part]
            keep[1, t, q] = outs[q][part : 2 * part]
            far_give[t, q] = outs[q][2 * part : 3 * part].astype(jnp.bfloat16)
            near_give[t, q] = outs[q][3 * part :].astype(jnp.bfloat16)
    for s in range(len(EARLY) * SLOTS):
        t = place(EARLY, s)
        for side in range(2):
            keep[side, t] = early_keep[side, s]
        far_give[t] = early_far[s]
        near_give[t] = early_near[s]
    for s in range(SLOTS):
        t = order[LAST * SLOTS + s]
        for side in range(2):
            keep[side, t] = jnp.zeros(keep.shape[2:], keep.dtype)
        far_give[t] = jnp.zeros(far_give.shape[1:], far_give.dtype)
        near_give[t] = jnp.zeros(near_give.shape[1:], near_give.dtype)


def mid(order, ops, blocks, staged, wdev, sdev):
    phys, part, blk = staged[0].shape[2:]
    n = len(blocks) * SLOTS
    give = jax.ShapeDtypeStruct((sdev, phys, part, blk), jnp.bfloat16)
    return pl.pallas_call(
        functools.partial(mid_kernel, wdev, sdev),
        out_shape=[jax.ShapeDtypeStruct((2, sdev, phys, part, blk), jnp.float32), give, give],
        in_specs=[space(pl.ANY)] * 2 + [space(pltpu.VMEM)] * (len(blocks) + 5),
        out_specs=[space(pltpu.VMEM)] * 3,
        scratch_shapes=[
            pltpu.SMEM(order.shape, order.dtype),
            pltpu.SMEM(ops.shape, ops.dtype),
            pltpu.SemaphoreType.DMA((2,)),
        ],
        compiler_params=params(),
        cost_estimate=pl.CostEstimate(
            flops=n * wdev * phys * blk**3 * 4,
            bytes_accessed=8 * 1024 * 1024,
            transcendentals=0,
        ),
        name="mid",
    )(order, ops, *blocks, *staged[3:5], *staged[:3])


def last_kernel(wdev, after, block, lstage, rstage, oprows, named, *gives):
    phys, blk = block.shape[2], block.shape[4]
    part = blk // len(gives)
    size = phys * part
    first = len(MID) * SLOTS
    me = lax.axis_index("sec")
    other = (jnp.bitwise_xor(me, LAST) > me).astype(jnp.int32)
    wides = []
    for s in range(SLOTS):
        wides.append(left_rows(lstage[first + s], [block[other, s, p] for p in range(phys)]))
    for s in range(SLOTS):
        outs = right_rows(wides[s], rstage[first + s], row_op(oprows, s, phys), wdev, phys)
        for i, m in enumerate(QUARTERS):
            for q in range(phys):
                rows = outs[q][i * part : (i + 1) * part].astype(gives[m].dtype)
                at = s * size + q * part
                gives[m][at : at + part] = rows
    for give in gives:
        give[SLOTS * size :] = named[...].astype(give.dtype)


def last(after, block, staged, wdev):
    phys, part, blk = staged[0].shape[2:]
    shape = (SLOTS * phys * part + NAME_ROWS, blk)
    give = jax.ShapeDtypeStruct(shape, jnp.bfloat16)
    return pl.pallas_call(
        functools.partial(last_kernel, wdev),
        out_shape=[jax.ShapeDtypeStruct(shape, jnp.float32)] + [give] * 3,
        in_specs=[space(pl.ANY)] + [space(pltpu.VMEM)] * 5,
        out_specs=[space(pltpu.VMEM)] * 4,
        compiler_params=params(),
        cost_estimate=pl.CostEstimate(
            flops=SLOTS * wdev * phys * blk**3 * 4,
            bytes_accessed=4 * 1024 * 1024,
            transcendentals=0,
        ),
        name="last",
    )(after, block, *staged[3:])


def pair_kernel(keep, got, out):
    out[...] = (keep[0] + got[...].astype(jnp.float32)).astype(out.dtype)


def pair(keep, got):
    return pl.pallas_call(
        pair_kernel,
        out_shape=jax.ShapeDtypeStruct(got.shape, got.dtype),
        in_specs=[space(pltpu.VMEM)] * 2,
        out_specs=space(pltpu.VMEM),
        compiler_params=params(),
        name="pair",
    )(keep, got)


def tail_sum(tails, t, first, count):
    total = None
    for tail in tails:
        end = tail.shape[0] - NAME_ROWS
        size = end // SLOTS
        names = tail[end:, :].astype(jnp.float32)
        for s in range(SLOTS):
            at = s * size + first
            rows = tail[at : at + count, :].astype(jnp.float32)
            value = jnp.where(names[s : s + 1] == t, rows, 0.0)
            total = value if total is None else total + value
    return total


def base_kernel(keep, near, far, own, mate, acc):
    sdev, phys, part, blk = acc.shape
    for t in range(sdev):
        total = keep[1, t] + near[t].astype(jnp.float32) + far[t].astype(jnp.float32)
        acc[t] = total + tail_sum((own, mate), t, 0, phys * part).reshape(phys, part, blk)


def base(keep, near, far, own, mate):
    return pl.pallas_call(
        base_kernel,
        out_shape=jax.ShapeDtypeStruct(far.shape, jnp.float32),
        in_specs=[space(pltpu.VMEM)] * 5,
        out_specs=space(pltpu.VMEM),
        compiler_params=params(),
        name="base",
    )(keep, near, far, own, mate)


def finish_kernel(total, tail2, tail3, out, acc):
    sdev, phys, part, blk = total.shape
    for t in range(sdev):
        late = tail_sum((tail2, tail3), t, 0, phys * part).reshape(phys, part, blk)
        acc[t] = total[t] + late
    for q in range(phys):
        out[:, q] = jnp.swapaxes(acc[:, q], 0, 1).astype(out.dtype)


def finish(total, tail2, tail3):
    sdev, phys, part, blk = total.shape
    return pl.pallas_call(
        finish_kernel,
        out_shape=jax.ShapeDtypeStruct((part, phys, sdev, blk), jnp.bfloat16),
        in_specs=[space(pltpu.VMEM)] * 3,
        out_specs=space(pltpu.VMEM),
        scratch_shapes=[pltpu.VMEM(total.shape, total.dtype)],
        compiler_params=params(),
        name="finish",
    )(total, tail2, tail3)


def fast_shards(psi, left_env, right_env, site_op, source):
    nsec = lax.axis_size("sec")
    nmpo = lax.axis_size("mpo")
    sdev = psi.shape[0]
    wdev = left_env.shape[0]
    blocks = jnp.transpose(psi, (0, 2, 1, 3))
    ops = site_op.astype(jnp.float32).reshape(-1)
    table = pltpu.with_memory_space_constraint(source, pltpu.HBM)
    pinned = pltpu.with_memory_space_constraint(blocks, pltpu.HBM)
    held = route(EARLY + MID + (LAST,), table, pinned)
    arrived = {0: held[0]}
    for k, value in zip(MID, held[len(EARLY) :]):
        arrived[k] = lax.ppermute(value, "sec", [(i, i ^ k) for i in range(nsec)])
    both = double(held[-1])
    order = receive_order(table, both, nsec, sdev)
    pairs = [[i, i ^ LAST] for i in range(nsec) if i < i ^ LAST]
    final = lax.all_to_all(both, "sec", 0, 0, axis_index_groups=pairs, tiled=True)

    def across(value, m):
        return lax.ppermute(value, "mpo", [(i, i ^ m) for i in range(nmpo)])

    staged = early(order, ops, [arrived[k] for k in EARLY], left_env, right_env, nsec, nmpo)
    keep, far_give, near_give = mid(order, ops, [arrived[k] for k in MID], staged, wdev, sdev)
    summed = pair(keep, across(far_give, 1))
    far = across(summed, 2)
    near = across(near_give, 1)
    own, give1, give2, give3 = last(summed, final, staged, wdev)
    total = base(keep, near, far, own, across(give1, 1))
    out = finish(total, across(give2, 2), across(give3, 3))
    return jnp.transpose(out, (0, 2, 1, 3))


def any_shards(psi, left_env, right_env, site_op, source):
    me_sec = lax.axis_index("sec")
    nsec = lax.axis_size("sec")
    sdev = psi.shape[0]
    blk = psi.shape[1]
    phys = psi.shape[2]
    slots = max(2, (sdev + nsec - 1) // nsec)
    table = source[0]
    owners = (table // sdev).reshape(nsec, sdev)
    mine = owners == me_sec
    ranked = jnp.cumsum(mine.astype(jnp.int32), axis=1) - 1
    picked = mine[:, None, :] & (
        ranked[:, None, :] == jnp.arange(slots, dtype=jnp.int32)[None, :, None]
    )
    local_rows = (table % sdev).reshape(nsec, sdev)
    chosen = jnp.sum(jnp.where(picked, local_rows[:, None, :], 0), axis=2)
    outgoing = jnp.take(psi, chosen.reshape(-1), axis=0).reshape(nsec, slots, blk, phys, blk)
    arrived = lax.all_to_all(outgoing, "sec", split_axis=0, concat_axis=0, tiled=True)
    my_sources = lax.dynamic_slice_in_dim(table, me_sec * sdev, sdev)
    sender = my_sources // sdev
    onehot = (sender[:, None] == jnp.arange(nsec, dtype=jnp.int32)[None, :]).astype(jnp.int32)
    slot_index = jnp.sum(jnp.cumsum(onehot, axis=0) * onehot, axis=1) - 1
    position = sender * slots + slot_index
    taken = jnp.take(arrived.reshape(nsec * slots, blk, phys, blk), position, axis=0)
    left = jnp.einsum(
        "wtab,tbpc->wtapc", left_env, taken, preferred_element_type=jnp.float32
    ).astype(jnp.bfloat16)
    mixed = jnp.einsum(
        "wtapc,wtpq->wtaqc", left, site_op, preferred_element_type=jnp.float32
    ).astype(jnp.bfloat16)
    partial_value = jnp.einsum(
        "wtaqc,wtcd->atqd", mixed, right_env, preferred_element_type=jnp.float32
    )
    summed = lax.psum_scatter(partial_value, "mpo", scatter_dimension=0, tiled=True)
    return summed.astype(jnp.bfloat16)


def shards(psi, left_env, right_env, site_op, source):
    nsec = lax.axis_size("sec")
    nmpo = lax.axis_size("mpo")
    exact = psi.shape[0] == SLOTS * nsec and nsec == 4 and nmpo == 4
    body = fast_shards if exact else any_shards
    return body(psi, left_env, right_env, site_op, source)


def solution(mesh):
    placed = (
        P(("grp", "sec"), None, None, None),
        P(("grp", "mpo"), "sec", None, None),
        P(("grp", "mpo"), "sec", None, None),
        P(("grp", "mpo"), "sec", None, None),
        P("mpo", None),
    )
    return jax.shard_map(
        shards,
        mesh=mesh,
        in_specs=placed,
        out_specs=P("mpo", ("grp", "sec"), None, None),
        check_vma=False,
    )
```

```python
import functools

import jax
import jax.numpy as jnp
from jax import lax
from jax.experimental import pallas as pl
from jax.experimental.pallas import tpu as pltpu
from jax.sharding import PartitionSpec as P

SLOTS = 2
EARLY = (0,)
MID = (2, 1)
LAST = 3
LATE = MID + (LAST,)
NAME_ROWS = 16
VMEM_BYTES = 16 * 1024 * 1024


def space(kind):
    return pl.BlockSpec(memory_space=kind)


def params():
    return pltpu.CompilerParams(vmem_limit_bytes=VMEM_BYTES)


def split(value, count):
    if count & (count - 1) == 0:
        shift = count.bit_length() - 1
        return jnp.right_shift(value, shift), jnp.bitwise_and(value, count - 1)
    owner = lax.div(value, jnp.int32(count))
    return owner, value - owner * count


def pick(table, base, count, block):
    zero = jnp.int32(0)
    seen, places, rows = zero, [zero, zero], [zero, zero]
    for t in range(count):
        owner, row = split(table[0, base + t], count)
        hit = owner == block
        for j in range(SLOTS):
            here = hit & (seen == j)
            places[j] = jnp.where(here, jnp.int32(t), places[j])
            rows[j] = jnp.where(here, row, rows[j])
        seen = seen + hit.astype(jnp.int32)
    return places, rows


def route_kernel(classes, source, psi, *refs):
    outs, (table, held, load, sems) = refs[: len(classes)], refs[len(classes) :]
    sdev = psi.shape[0]
    me = lax.axis_index("sec")
    fetch = pltpu.make_async_copy(source, table, load)
    fetch.start()
    copies = []
    copy = pltpu.make_async_copy(psi, held, sems.at[0])
    copy.start()
    copies.append(copy)
    fetch.wait()
    rows = [pick(table, jnp.bitwise_xor(me, k) * sdev, sdev, me)[1] for k in classes]
    for copy in copies:
        copy.wait()
    for i in range(len(classes)):
        for j in range(SLOTS):
            outs[i][j] = held[rows[i][j]]


def route(classes, source, psi):
    block = psi.shape[1:]
    return pl.pallas_call(
        functools.partial(route_kernel, classes),
        out_shape=[jax.ShapeDtypeStruct((SLOTS,) + block, psi.dtype)] * len(classes),
        in_specs=[space(pl.ANY)] * 2,
        out_specs=[space(pltpu.VMEM)] * len(classes),
        scratch_shapes=[
            pltpu.SMEM(source.shape, jnp.int32),
            pltpu.VMEM(psi.shape, psi.dtype),
            pltpu.SemaphoreType.DMA,
            pltpu.SemaphoreType.DMA((1,)),
        ],
        compiler_params=params(),
        name="route",
    )(source, psi)


def double_kernel(block, after, out, sems):
    copies = [pltpu.make_async_copy(block, out.at[i], sems.at[i]) for i in range(2)]
    for copy in copies:
        copy.start()
    for copy in copies:
        copy.wait()


def double(block, after):
    return pl.pallas_call(
        double_kernel,
        out_shape=jax.ShapeDtypeStruct((2,) + block.shape, block.dtype),
        in_specs=[space(pltpu.VMEM), space(pl.ANY)],
        out_specs=space(pl.ANY),
        scratch_shapes=[pltpu.SemaphoreType.DMA((2,))],
        compiler_params=params(),
        name="double",
    )(block, after)


def order_kernel(nsec, sdev, source, after, order, table, load):
    me = lax.axis_index("sec")
    fetch = pltpu.make_async_copy(source, table, load)
    fetch.start()
    fetch.wait()
    for k in range(nsec):
        places = pick(table, me * sdev, sdev, jnp.bitwise_xor(me, k))[0]
        for j in range(SLOTS):
            order[k * SLOTS + j] = places[j]


def receive_order(source, after, nsec, sdev):
    return pl.pallas_call(
        functools.partial(order_kernel, nsec, sdev),
        out_shape=jax.ShapeDtypeStruct((nsec * SLOTS,), jnp.int32),
        in_specs=[space(pl.ANY)] * 2,
        out_specs=space(pltpu.SMEM),
        scratch_shapes=[pltpu.SMEM(source.shape, jnp.int32), pltpu.SemaphoreType.DMA],
        compiler_params=params(),
        name="order",
    )(source, after)


def left_rows(lhs, block):
    wide = jnp.dot(lhs, jnp.concatenate(block, axis=1), preferred_element_type=jnp.float32)
    return wide.astype(jnp.bfloat16)


def right_rows(wide, rhs, op, wdev, phys):
    rows = wide.shape[0] // wdev
    blk = rhs.shape[1]
    outs = []
    for q in range(phys):
        across = []
        for w in range(wdev):
            total = None
            for p in range(phys):
                part = wide[w * rows : (w + 1) * rows, p * blk : (p + 1) * blk]
                term = part.astype(jnp.float32) * op(w, p, q)
                total = term if total is None else total + term
            across.append(total.astype(jnp.bfloat16))
        mixed = jnp.concatenate(across, axis=1)
        outs.append(jnp.dot(mixed, rhs, preferred_element_type=jnp.float32))
    return outs


def scalar_op(ops, t, sdev, phys):
    return lambda w, p, q: ops[(w * sdev + t) * (phys * phys) + p * phys + q]


def row_op(rows, s, phys):
    def op(w, p, q):
        i = (w * phys + p) * phys + q
        return rows[s, i : i + 1, :]

    return op


QUARTERS = (2, 0, 3, 1)


def early_kernel(nsec, nmpo, order, ops, *refs):
    blocks, refs = refs[: len(EARLY)], refs[len(EARLY) :]
    left, right, keep, far_give, near_give, lstage, rstage, oprows, named = refs
    wdev, sdev, blk = left.shape[:3]
    phys = blocks[0].shape[1]
    part = blk // nmpo
    me = lax.axis_index("mpo")

    def side(t):
        rows = []
        for w in range(wdev):
            for m in QUARTERS:
                start = pl.multiple_of(jnp.bitwise_xor(me, m) * part, part)
                rows.append(left[w, t, pl.ds(start, part), :])
        return jnp.concatenate(rows, axis=0)

    for s in range(len(LATE) * SLOTS):
        t = order[LATE[s // SLOTS] * SLOTS + s % SLOTS]
        lstage[s] = side(t)
        rstage[s] = right[:, t].reshape(wdev * blk, blk)
    line = lax.broadcasted_iota(jnp.int32, named.shape, 0)
    names = jnp.zeros(named.shape, jnp.float32)
    for s in range(SLOTS):
        t = order[LAST * SLOTS + s]
        names = jnp.where(line == s, t.astype(jnp.float32), names)
        op = scalar_op(ops, t, sdev, phys)
        for w in range(wdev):
            for p in range(phys):
                for q in range(phys):
                    i = (w * phys + p) * phys + q
                    oprows[s, i : i + 1, :] = jnp.full((1, blk), op(w, p, q), jnp.float32)
    named[...] = names.astype(named.dtype)
    for i, k in enumerate(EARLY):
        for j in range(SLOTS):
            s = i * SLOTS + j
            t = order[k * SLOTS + j]
            rhs = right[:, t].reshape(wdev * blk, blk)
            block = [blocks[i][j, p] for p in range(phys)]
            op = scalar_op(ops, t, sdev, phys)
            outs = right_rows(left_rows(side(t), block), rhs, op, wdev, phys)
            for q in range(phys):
                keep[0, s, q] = outs[q][:part]
                keep[1, s, q] = outs[q][part : 2 * part]
                far_give[s, q] = outs[q][2 * part : 3 * part].astype(jnp.bfloat16)
                near_give[s, q] = outs[q][3 * part :].astype(jnp.bfloat16)


def early(order, ops, blocks, left, right, nsec, nmpo):
    wdev, sdev, blk = left.shape[:3]
    phys = blocks[0].shape[1]
    part = blk // nmpo
    n, late_n = len(EARLY) * SLOTS, len(LATE) * SLOTS
    keep = jax.ShapeDtypeStruct((2, n, phys, part, blk), jnp.float32)
    give = jax.ShapeDtypeStruct((n, phys, part, blk), jnp.bfloat16)
    rows = jax.ShapeDtypeStruct((SLOTS, wdev * phys * phys, blk), jnp.float32)
    name = jax.ShapeDtypeStruct((NAME_ROWS, blk), jnp.bfloat16)
    whole = jax.ShapeDtypeStruct((late_n, wdev * blk, blk), jnp.bfloat16)
    return pl.pallas_call(
        functools.partial(early_kernel, nsec, nmpo),
        out_shape=[keep, give, give, whole, whole, rows, name],
        in_specs=[space(pltpu.SMEM)] * 2 + [space(pltpu.VMEM)] * (len(EARLY) + 2),
        out_specs=[space(pltpu.VMEM)] * 7,
        compiler_params=params(),
        cost_estimate=pl.CostEstimate(
            flops=n * wdev * phys * blk**3 * 4,
            bytes_accessed=8 * 1024 * 1024,
            transcendentals=0,
        ),
        name="early",
    )(order, ops, *blocks, left, right)


def mid_kernel(wdev, sdev, order_in, ops_in, *refs):
    nmid = len(MID)
    blocks, refs = refs[:nmid], refs[nmid:]
    lstage, rstage, early_keep, early_far, early_near, keep, far_give, near_give = refs[:8]
    order, ops, sems = refs[8:]
    phys, part = far_give.shape[1], far_give.shape[2]
    loads = [
        pltpu.make_async_copy(order_in, order, sems.at[0]),
        pltpu.make_async_copy(ops_in, ops, sems.at[1]),
    ]
    for load in loads:
        load.start()
    wides = []
    for s in range(nmid * SLOTS):
        block = [blocks[s // SLOTS][s % SLOTS, p] for p in range(phys)]
        wides.append(left_rows(lstage[s], block))
    for load in loads:
        load.wait()

    def place(classes, s):
        return order[classes[s // SLOTS] * SLOTS + s % SLOTS]

    for s in range(nmid * SLOTS):
        t = place(MID, s)
        outs = right_rows(wides[s], rstage[s], scalar_op(ops, t, sdev, phys), wdev, phys)
        for q in range(phys):
            keep[0, t, q] = outs[q][:part]
            keep[1, t, q] = outs[q][part : 2 * part]
            far_give[t, q] = outs[q][2 * part : 3 * part].astype(jnp.bfloat16)
            near_give[t, q] = outs[q][3 * part :].astype(jnp.bfloat16)
    for s in range(len(EARLY) * SLOTS):
        t = place(EARLY, s)
        for side in range(2):
            keep[side, t] = early_keep[side, s]
        far_give[t] = early_far[s]
        near_give[t] = early_near[s]
    for s in range(SLOTS):
        t = order[LAST * SLOTS + s]
        for side in range(2):
            keep[side, t] = jnp.zeros(keep.shape[2:], keep.dtype)
        far_give[t] = jnp.zeros(far_give.shape[1:], far_give.dtype)
        near_give[t] = jnp.zeros(near_give.shape[1:], near_give.dtype)


def mid(order, ops, blocks, staged, wdev, sdev):
    phys, part, blk = staged[0].shape[2:]
    n = len(blocks) * SLOTS
    give = jax.ShapeDtypeStruct((sdev, phys, part, blk), jnp.bfloat16)
    return pl.pallas_call(
        functools.partial(mid_kernel, wdev, sdev),
        out_shape=[jax.ShapeDtypeStruct((2, sdev, phys, part, blk), jnp.float32), give, give],
        in_specs=[space(pl.ANY)] * 2 + [space(pltpu.VMEM)] * (len(blocks) + 5),
        out_specs=[space(pltpu.VMEM)] * 3,
        scratch_shapes=[
            pltpu.SMEM(order.shape, order.dtype),
            pltpu.SMEM(ops.shape, ops.dtype),
            pltpu.SemaphoreType.DMA((2,)),
        ],
        compiler_params=params(),
        cost_estimate=pl.CostEstimate(
            flops=n * wdev * phys * blk**3 * 4,
            bytes_accessed=8 * 1024 * 1024,
            transcendentals=0,
        ),
        name="mid",
    )(order, ops, *blocks, *staged[3:5], *staged[:3])


def last_kernel(wdev, after, block, lstage, rstage, oprows, named, *gives):
    phys, blk = block.shape[2], block.shape[4]
    part = blk // len(gives)
    size = phys * part
    first = len(MID) * SLOTS
    me = lax.axis_index("sec")
    other = (jnp.bitwise_xor(me, LAST) > me).astype(jnp.int32)
    wides = []
    for s in range(SLOTS):
        wides.append(left_rows(lstage[first + s], [block[other, s, p] for p in range(phys)]))
    for s in range(SLOTS):
        outs = right_rows(wides[s], rstage[first + s], row_op(oprows, s, phys), wdev, phys)
        for i, m in enumerate(QUARTERS):
            for q in range(phys):
                rows = outs[q][i * part : (i + 1) * part].astype(gives[m].dtype)
                at = s * size + q * part
                gives[m][at : at + part] = rows
    for give in gives:
        give[SLOTS * size :] = named[...].astype(give.dtype)


def last(after, block, staged, wdev):
    phys, part, blk = staged[0].shape[2:]
    shape = (SLOTS * phys * part + NAME_ROWS, blk)
    give = jax.ShapeDtypeStruct(shape, jnp.bfloat16)
    return pl.pallas_call(
        functools.partial(last_kernel, wdev),
        out_shape=[jax.ShapeDtypeStruct(shape, jnp.float32)] + [give] * 3,
        in_specs=[space(pl.ANY)] + [space(pltpu.VMEM)] * 5,
        out_specs=[space(pltpu.VMEM)] * 4,
        compiler_params=params(),
        cost_estimate=pl.CostEstimate(
            flops=SLOTS * wdev * phys * blk**3 * 4,
            bytes_accessed=4 * 1024 * 1024,
            transcendentals=0,
        ),
        name="last",
    )(after, block, *staged[3:])


def pair_kernel(keep, got, out):
    out[...] = (keep[0] + got[...].astype(jnp.float32)).astype(out.dtype)


def pair(keep, got):
    return pl.pallas_call(
        pair_kernel,
        out_shape=jax.ShapeDtypeStruct(got.shape, got.dtype),
        in_specs=[space(pltpu.VMEM)] * 2,
        out_specs=space(pltpu.VMEM),
        compiler_params=params(),
        name="pair",
    )(keep, got)


def tail_sum(tails, t, first, count):
    total = None
    for tail in tails:
        end = tail.shape[0] - NAME_ROWS
        size = end // SLOTS
        names = tail[end:, :].astype(jnp.float32)
        for s in range(SLOTS):
            at = s * size + first
            rows = tail[at : at + count, :].astype(jnp.float32)
            value = jnp.where(names[s : s + 1] == t, rows, 0.0)
            total = value if total is None else total + value
    return total


def base_kernel(keep, near, far, own, mate, acc):
    sdev, phys, part, blk = acc.shape
    for t in range(sdev):
        total = keep[1, t] + near[t].astype(jnp.float32) + far[t].astype(jnp.float32)
        acc[t] = total + tail_sum((own, mate), t, 0, phys * part).reshape(phys, part, blk)


def base(keep, near, far, own, mate):
    return pl.pallas_call(
        base_kernel,
        out_shape=jax.ShapeDtypeStruct(far.shape, jnp.float32),
        in_specs=[space(pltpu.VMEM)] * 5,
        out_specs=space(pltpu.VMEM),
        compiler_params=params(),
        name="base",
    )(keep, near, far, own, mate)


def finish_kernel(total, tail2, tail3, out, acc):
    sdev, phys, part, blk = total.shape
    for t in range(sdev):
        late = tail_sum((tail2, tail3), t, 0, phys * part).reshape(phys, part, blk)
        acc[t] = total[t] + late
    for q in range(phys):
        out[:, q] = jnp.swapaxes(acc[:, q], 0, 1).astype(out.dtype)


def finish(total, tail2, tail3):
    sdev, phys, part, blk = total.shape
    return pl.pallas_call(
        finish_kernel,
        out_shape=jax.ShapeDtypeStruct((part, phys, sdev, blk), jnp.bfloat16),
        in_specs=[space(pltpu.VMEM)] * 3,
        out_specs=space(pltpu.VMEM),
        scratch_shapes=[pltpu.VMEM(total.shape, total.dtype)],
        compiler_params=params(),
        name="finish",
    )(total, tail2, tail3)


def fast_shards(psi, left_env, right_env, site_op, source):
    nsec = lax.axis_size("sec")
    nmpo = lax.axis_size("mpo")
    sdev = psi.shape[0]
    wdev = left_env.shape[0]
    blocks = jnp.transpose(psi, (0, 2, 1, 3))
    ops = site_op.astype(jnp.float32).reshape(-1)
    table = pltpu.with_memory_space_constraint(source, pltpu.HBM)
    pinned = pltpu.with_memory_space_constraint(blocks, pltpu.HBM)
    held = route(EARLY + MID + (LAST,), table, pinned)
    arrived = {0: held[0]}
    for k, value in zip(MID, held[len(EARLY) :]):
        arrived[k] = lax.ppermute(value, "sec", [(i, i ^ k) for i in range(nsec)])
    order = receive_order(table, held[0], nsec, sdev)
    both = double(held[-1], order)
    pairs = [[i, i ^ LAST] for i in range(nsec) if i < i ^ LAST]
    final = lax.all_to_all(both, "sec", 0, 0, axis_index_groups=pairs, tiled=True)

    def across(value, m):
        return lax.ppermute(value, "mpo", [(i, i ^ m) for i in range(nmpo)])

    staged = early(order, ops, [arrived[k] for k in EARLY], left_env, right_env, nsec, nmpo)
    keep, far_give, near_give = mid(order, ops, [arrived[k] for k in MID], staged, wdev, sdev)
    summed = pair(keep, across(far_give, 1))
    far = across(summed, 2)
    near = across(near_give, 1)
    own, give1, give2, give3 = last(summed, final, staged, wdev)
    total = base(keep, near, far, own, across(give1, 1))
    out = finish(total, across(give2, 2), across(give3, 3))
    return jnp.transpose(out, (0, 2, 1, 3))


def any_shards(psi, left_env, right_env, site_op, source):
    me_sec = lax.axis_index("sec")
    nsec = lax.axis_size("sec")
    sdev = psi.shape[0]
    blk = psi.shape[1]
    phys = psi.shape[2]
    slots = max(2, (sdev + nsec - 1) // nsec)
    table = source[0]
    owners = (table // sdev).reshape(nsec, sdev)
    mine = owners == me_sec
    ranked = jnp.cumsum(mine.astype(jnp.int32), axis=1) - 1
    picked = mine[:, None, :] & (
        ranked[:, None, :] == jnp.arange(slots, dtype=jnp.int32)[None, :, None]
    )
    local_rows = (table % sdev).reshape(nsec, sdev)
    chosen = jnp.sum(jnp.where(picked, local_rows[:, None, :], 0), axis=2)
    outgoing = jnp.take(psi, chosen.reshape(-1), axis=0).reshape(nsec, slots, blk, phys, blk)
    arrived = lax.all_to_all(outgoing, "sec", split_axis=0, concat_axis=0, tiled=True)
    my_sources = lax.dynamic_slice_in_dim(table, me_sec * sdev, sdev)
    sender = my_sources // sdev
    onehot = (sender[:, None] == jnp.arange(nsec, dtype=jnp.int32)[None, :]).astype(jnp.int32)
    slot_index = jnp.sum(jnp.cumsum(onehot, axis=0) * onehot, axis=1) - 1
    position = sender * slots + slot_index
    taken = jnp.take(arrived.reshape(nsec * slots, blk, phys, blk), position, axis=0)
    left = jnp.einsum(
        "wtab,tbpc->wtapc", left_env, taken, preferred_element_type=jnp.float32
    ).astype(jnp.bfloat16)
    mixed = jnp.einsum(
        "wtapc,wtpq->wtaqc", left, site_op, preferred_element_type=jnp.float32
    ).astype(jnp.bfloat16)
    partial_value = jnp.einsum(
        "wtaqc,wtcd->atqd", mixed, right_env, preferred_element_type=jnp.float32
    )
    summed = lax.psum_scatter(partial_value, "mpo", scatter_dimension=0, tiled=True)
    return summed.astype(jnp.bfloat16)


def shards(psi, left_env, right_env, site_op, source):
    nsec = lax.axis_size("sec")
    nmpo = lax.axis_size("mpo")
    exact = psi.shape[0] == SLOTS * nsec and nsec == 4 and nmpo == 4
    body = fast_shards if exact else any_shards
    return body(psi, left_env, right_env, site_op, source)


def solution(mesh):
    placed = (
        P(("grp", "sec"), None, None, None),
        P(("grp", "mpo"), "sec", None, None),
        P(("grp", "mpo"), "sec", None, None),
        P(("grp", "mpo"), "sec", None, None),
        P("mpo", None),
    )
    return jax.shard_map(
        shards,
        mesh=mesh,
        in_specs=placed,
        out_specs=P("mpo", ("grp", "sec"), None, None),
        check_vma=False,
    )
```

```python
import functools

import jax
import jax.numpy as jnp
from jax import lax
from jax.experimental import pallas as pl
from jax.experimental.pallas import tpu as pltpu
from jax.sharding import PartitionSpec as P

SLOTS = 2
EARLY = (0,)
MID = (2, 1)
LAST = 3
LATE = MID + (LAST,)
NAME_ROWS = 16
VMEM_BYTES = 16 * 1024 * 1024


def space(kind):
    return pl.BlockSpec(memory_space=kind)


def params():
    return pltpu.CompilerParams(vmem_limit_bytes=VMEM_BYTES)


def split(value, count):
    if count & (count - 1) == 0:
        shift = count.bit_length() - 1
        return jnp.right_shift(value, shift), jnp.bitwise_and(value, count - 1)
    owner = lax.div(value, jnp.int32(count))
    return owner, value - owner * count


def pick(table, base, count, block):
    zero = jnp.int32(0)
    seen, places, rows = zero, [zero, zero], [zero, zero]
    for t in range(count):
        owner, row = split(table[0, base + t], count)
        hit = owner == block
        for j in range(SLOTS):
            here = hit & (seen == j)
            places[j] = jnp.where(here, jnp.int32(t), places[j])
            rows[j] = jnp.where(here, row, rows[j])
        seen = seen + hit.astype(jnp.int32)
    return places, rows


def route_kernel(classes, source, psi, *refs):
    outs, (table, held, load, sems) = refs[: len(classes)], refs[len(classes) :]
    sdev = psi.shape[0]
    me = lax.axis_index("sec")
    fetch = pltpu.make_async_copy(source, table, load)
    fetch.start()
    copies = []
    copy = pltpu.make_async_copy(psi, held, sems.at[0])
    copy.start()
    copies.append(copy)
    fetch.wait()
    rows = [pick(table, jnp.bitwise_xor(me, k) * sdev, sdev, me)[1] for k in classes]
    for copy in copies:
        copy.wait()
    for i in range(len(classes)):
        for j in range(SLOTS):
            outs[i][j] = held[rows[i][j]]


def route(classes, source, psi):
    block = psi.shape[1:]
    return pl.pallas_call(
        functools.partial(route_kernel, classes),
        out_shape=[jax.ShapeDtypeStruct((SLOTS,) + block, psi.dtype)] * len(classes),
        in_specs=[space(pl.ANY)] * 2,
        out_specs=[space(pltpu.VMEM)] * len(classes),
        scratch_shapes=[
            pltpu.SMEM(source.shape, jnp.int32),
            pltpu.VMEM(psi.shape, psi.dtype),
            pltpu.SemaphoreType.DMA,
            pltpu.SemaphoreType.DMA((1,)),
        ],
        compiler_params=params(),
        name="route",
    )(source, psi)


def double_kernel(block, after, out, sems):
    copies = [pltpu.make_async_copy(block, out.at[i], sems.at[i]) for i in range(2)]
    for copy in copies:
        copy.start()
    for copy in copies:
        copy.wait()


def double(block, after):
    return pl.pallas_call(
        double_kernel,
        out_shape=jax.ShapeDtypeStruct((2,) + block.shape, block.dtype),
        in_specs=[space(pltpu.VMEM), space(pl.ANY)],
        out_specs=space(pl.ANY),
        scratch_shapes=[pltpu.SemaphoreType.DMA((2,))],
        compiler_params=params(),
        name="double",
    )(block, after)


def order_kernel(nsec, sdev, source, after, order, table, load):
    me = lax.axis_index("sec")
    fetch = pltpu.make_async_copy(source, table, load)
    fetch.start()
    fetch.wait()
    for k in range(nsec):
        places = pick(table, me * sdev, sdev, jnp.bitwise_xor(me, k))[0]
        for j in range(SLOTS):
            order[k * SLOTS + j] = places[j]


def receive_order(source, after, nsec, sdev):
    return pl.pallas_call(
        functools.partial(order_kernel, nsec, sdev),
        out_shape=jax.ShapeDtypeStruct((nsec * SLOTS,), jnp.int32),
        in_specs=[space(pl.ANY)] * 2,
        out_specs=space(pltpu.SMEM),
        scratch_shapes=[pltpu.SMEM(source.shape, jnp.int32), pltpu.SemaphoreType.DMA],
        compiler_params=params(),
        name="order",
    )(source, after)


def left_rows(lhs, block):
    wide = jnp.dot(lhs, jnp.concatenate(block, axis=1), preferred_element_type=jnp.float32)
    return wide.astype(jnp.bfloat16)


def right_rows(wide, rhs, op, wdev, phys):
    rows = wide.shape[0] // wdev
    blk = rhs.shape[1]
    outs = []
    for q in range(phys):
        across = []
        for w in range(wdev):
            total = None
            for p in range(phys):
                part = wide[w * rows : (w + 1) * rows, p * blk : (p + 1) * blk]
                term = part.astype(jnp.float32) * op(w, p, q)
                total = term if total is None else total + term
            across.append(total.astype(jnp.bfloat16))
        mixed = jnp.concatenate(across, axis=1)
        outs.append(jnp.dot(mixed, rhs, preferred_element_type=jnp.float32))
    return outs


def scalar_op(ops, t, sdev, phys):
    return lambda w, p, q: ops[(w * sdev + t) * (phys * phys) + p * phys + q]


def row_op(rows, s, phys):
    def op(w, p, q):
        i = (w * phys + p) * phys + q
        return rows[s, i : i + 1, :]

    return op


QUARTERS = (2, 0, 3, 1)


def early_kernel(nsec, nmpo, order, ops, *refs):
    blocks, refs = refs[: len(EARLY)], refs[len(EARLY) :]
    left, right, keep, far_give, near_give, lstage, rstage, oprows, named = refs
    wdev, sdev, blk = left.shape[:3]
    phys = blocks[0].shape[1]
    part = blk // nmpo
    me = lax.axis_index("mpo")

    def side(t):
        rows = []
        for w in range(wdev):
            for m in QUARTERS:
                start = pl.multiple_of(jnp.bitwise_xor(me, m) * part, part)
                rows.append(left[w, t, pl.ds(start, part), :])
        return jnp.concatenate(rows, axis=0)

    for s in range(len(LATE) * SLOTS):
        t = order[LATE[s // SLOTS] * SLOTS + s % SLOTS]
        lstage[s] = side(t)
        rstage[s] = right[:, t].reshape(wdev * blk, blk)
    line = lax.broadcasted_iota(jnp.int32, named.shape, 0)
    names = jnp.zeros(named.shape, jnp.float32)
    for s in range(SLOTS):
        t = order[LAST * SLOTS + s]
        names = jnp.where(line == s, t.astype(jnp.float32), names)
        op = scalar_op(ops, t, sdev, phys)
        for w in range(wdev):
            for p in range(phys):
                for q in range(phys):
                    i = (w * phys + p) * phys + q
                    oprows[s, i : i + 1, :] = jnp.full((1, blk), op(w, p, q), jnp.float32)
    named[...] = names.astype(named.dtype)
    for i, k in enumerate(EARLY):
        for j in range(SLOTS):
            s = i * SLOTS + j
            t = order[k * SLOTS + j]
            rhs = right[:, t].reshape(wdev * blk, blk)
            block = [blocks[i][j, p] for p in range(phys)]
            op = scalar_op(ops, t, sdev, phys)
            outs = right_rows(left_rows(side(t), block), rhs, op, wdev, phys)
            for q in range(phys):
                keep[0, s, q] = outs[q][:part]
                keep[1, s, q] = outs[q][part : 2 * part]
                far_give[s, q] = outs[q][2 * part : 3 * part].astype(jnp.bfloat16)
                near_give[s, q] = outs[q][3 * part :].astype(jnp.bfloat16)


def early(order, ops, blocks, left, right, nsec, nmpo):
    wdev, sdev, blk = left.shape[:3]
    phys = blocks[0].shape[1]
    part = blk // nmpo
    n, late_n = len(EARLY) * SLOTS, len(LATE) * SLOTS
    keep = jax.ShapeDtypeStruct((2, n, phys, part, blk), jnp.float32)
    give = jax.ShapeDtypeStruct((n, phys, part, blk), jnp.bfloat16)
    rows = jax.ShapeDtypeStruct((SLOTS, wdev * phys * phys, blk), jnp.float32)
    name = jax.ShapeDtypeStruct((NAME_ROWS, blk), jnp.bfloat16)
    whole = jax.ShapeDtypeStruct((late_n, wdev * blk, blk), jnp.bfloat16)
    return pl.pallas_call(
        functools.partial(early_kernel, nsec, nmpo),
        out_shape=[keep, give, give, whole, whole, rows, name],
        in_specs=[space(pltpu.SMEM)] * 2 + [space(pltpu.VMEM)] * (len(EARLY) + 2),
        out_specs=[space(pltpu.VMEM)] * 7,
        compiler_params=params(),
        cost_estimate=pl.CostEstimate(
            flops=n * wdev * phys * blk**3 * 4,
            bytes_accessed=8 * 1024 * 1024,
            transcendentals=0,
        ),
        name="early",
    )(order, ops, *blocks, left, right)


def mid_kernel(wdev, sdev, order_in, ops_in, *refs):
    nmid = len(MID)
    blocks, refs = refs[:nmid], refs[nmid:]
    lstage, rstage, named, early_keep, early_far, early_near = refs[:6]
    keep, far_give, near_give, order, ops, sems = refs[6:]
    phys, part, blk = near_give.shape[1:]
    size = phys * part
    loads = [
        pltpu.make_async_copy(order_in, order, sems.at[0]),
        pltpu.make_async_copy(ops_in, ops, sems.at[1]),
    ]
    for load in loads:
        load.start()
    wides = []
    for s in range(nmid * SLOTS):
        block = [blocks[s // SLOTS][s % SLOTS, p] for p in range(phys)]
        wides.append(left_rows(lstage[s], block))
    for load in loads:
        load.wait()

    def place(classes, s):
        return order[classes[s // SLOTS] * SLOTS + s % SLOTS]

    for s in range(nmid * SLOTS):
        t = place(MID, s)
        outs = right_rows(wides[s], rstage[s], scalar_op(ops, t, sdev, phys), wdev, phys)
        for q in range(phys):
            keep[0, t, q] = outs[q][:part]
            keep[1, t, q] = outs[q][part : 2 * part]
            at = pl.multiple_of(t * size + q * part, part)
            far_give[pl.ds(at, part), :] = outs[q][2 * part : 3 * part].astype(jnp.bfloat16)
            near_give[t, q] = outs[q][3 * part :].astype(jnp.bfloat16)
    for s in range(len(EARLY) * SLOTS):
        t = place(EARLY, s)
        for side in range(2):
            keep[side, t] = early_keep[side, s]
        at = pl.multiple_of(t * size, size)
        far_give[pl.ds(at, size), :] = early_far[s].reshape(size, blk)
        near_give[t] = early_near[s]
    for s in range(SLOTS):
        t = order[LAST * SLOTS + s]
        for side in range(2):
            keep[side, t] = jnp.zeros(keep.shape[2:], keep.dtype)
        at = pl.multiple_of(t * size, size)
        far_give[pl.ds(at, size), :] = jnp.zeros((size, blk), far_give.dtype)
        near_give[t] = jnp.zeros(near_give.shape[1:], near_give.dtype)
    far_give[sdev * size :, :] = named[...]


def mid(order, ops, blocks, staged, wdev, sdev):
    phys, part, blk = staged[0].shape[2:]
    n = len(blocks) * SLOTS
    give = jax.ShapeDtypeStruct((sdev, phys, part, blk), jnp.bfloat16)
    flat = jax.ShapeDtypeStruct((sdev * phys * part + NAME_ROWS, blk), jnp.bfloat16)
    return pl.pallas_call(
        functools.partial(mid_kernel, wdev, sdev),
        out_shape=[jax.ShapeDtypeStruct((2, sdev, phys, part, blk), jnp.float32), flat, give],
        in_specs=[space(pl.ANY)] * 2 + [space(pltpu.VMEM)] * (len(blocks) + 6),
        out_specs=[space(pltpu.VMEM)] * 3,
        scratch_shapes=[
            pltpu.SMEM(order.shape, order.dtype),
            pltpu.SMEM(ops.shape, ops.dtype),
            pltpu.SemaphoreType.DMA((2,)),
        ],
        compiler_params=params(),
        cost_estimate=pl.CostEstimate(
            flops=n * wdev * phys * blk**3 * 4,
            bytes_accessed=8 * 1024 * 1024,
            transcendentals=0,
        ),
        name="mid",
    )(order, ops, *blocks, *staged[3:5], staged[6], *staged[:3])


def last_kernel(wdev, after, block, lstage, rstage, oprows, named, *gives):
    phys, blk = block.shape[2], block.shape[4]
    part = blk // len(gives)
    size = phys * part
    first = len(MID) * SLOTS
    me = lax.axis_index("sec")
    other = (jnp.bitwise_xor(me, LAST) > me).astype(jnp.int32)
    wides = []
    for s in range(SLOTS):
        wides.append(left_rows(lstage[first + s], [block[other, s, p] for p in range(phys)]))
    for s in range(SLOTS):
        outs = right_rows(wides[s], rstage[first + s], row_op(oprows, s, phys), wdev, phys)
        for i, m in enumerate(QUARTERS):
            for q in range(phys):
                rows = outs[q][i * part : (i + 1) * part].astype(gives[m].dtype)
                at = s * size + q * part
                gives[m][at : at + part] = rows
    for give in gives[:2]:
        give[SLOTS * size :] = named[...].astype(give.dtype)


def last(after, block, staged, wdev):
    phys, part, blk = staged[0].shape[2:]
    size = SLOTS * phys * part
    shape = (size + NAME_ROWS, blk)
    give = jax.ShapeDtypeStruct(shape, jnp.bfloat16)
    plain = jax.ShapeDtypeStruct((size, blk), jnp.bfloat16)
    return pl.pallas_call(
        functools.partial(last_kernel, wdev),
        out_shape=[jax.ShapeDtypeStruct(shape, jnp.float32), give, plain, plain],
        in_specs=[space(pl.ANY)] + [space(pltpu.VMEM)] * 5,
        out_specs=[space(pltpu.VMEM)] * 4,
        compiler_params=params(),
        cost_estimate=pl.CostEstimate(
            flops=SLOTS * wdev * phys * blk**3 * 4,
            bytes_accessed=4 * 1024 * 1024,
            transcendentals=0,
        ),
        name="last",
    )(after, block, *staged[3:])


def pair_kernel(keep, got, named, out):
    rows = got.shape[0] - NAME_ROWS
    own = keep[0].reshape(rows, out.shape[1])
    out[:rows, :] = (own + got[:rows, :].astype(jnp.float32)).astype(out.dtype)
    out[rows : rows + NAME_ROWS, :] = named[...]
    out[rows + NAME_ROWS :, :] = got[rows:, :]


def pair(keep, got, named):
    return pl.pallas_call(
        pair_kernel,
        out_shape=jax.ShapeDtypeStruct((got.shape[0] + NAME_ROWS, got.shape[1]), got.dtype),
        in_specs=[space(pltpu.VMEM)] * 3,
        out_specs=space(pltpu.VMEM),
        compiler_params=params(),
        name="pair",
    )(keep, got, named)


def tail_sum(tails, t):
    total = None
    for rows, names in tails:
        size = rows.shape[0] // SLOTS
        for s in range(SLOTS):
            part = rows[s * size : (s + 1) * size]
            value = jnp.where(names[s : s + 1] == t, part.astype(jnp.float32), 0.0)
            total = value if total is None else total + value
    return total


def base_kernel(keep, near, far, own, mate, acc):
    sdev, phys, part, blk = acc.shape
    size = phys * part
    end = SLOTS * size
    tails = [(tail[:end, :], tail[end:, :].astype(jnp.float32)) for tail in (own, mate)]
    for t in range(sdev):
        over = far[t * size : (t + 1) * size, :].astype(jnp.float32).reshape(phys, part, blk)
        total = keep[1, t] + near[t].astype(jnp.float32) + over
        acc[t] = total + tail_sum(tails, t).reshape(phys, part, blk)


def base(keep, near, far, own, mate):
    return pl.pallas_call(
        base_kernel,
        out_shape=jax.ShapeDtypeStruct(near.shape, jnp.float32),
        in_specs=[space(pltpu.VMEM)] * 5,
        out_specs=space(pltpu.VMEM),
        compiler_params=params(),
        name="base",
    )(keep, near, far, own, mate)


def finish_kernel(total, far, tail2, tail3, out, acc):
    sdev, phys, part, blk = total.shape
    at = sdev * phys * part
    names = far[at:, :].astype(jnp.float32)
    tails = [(tail2[...], names[:NAME_ROWS]), (tail3[...], names[NAME_ROWS:])]
    for t in range(sdev):
        acc[t] = total[t] + tail_sum(tails, t).reshape(phys, part, blk)
    for q in range(phys):
        out[:, q] = jnp.swapaxes(acc[:, q], 0, 1).astype(out.dtype)


def finish(total, far, tail2, tail3):
    sdev, phys, part, blk = total.shape
    return pl.pallas_call(
        finish_kernel,
        out_shape=jax.ShapeDtypeStruct((part, phys, sdev, blk), jnp.bfloat16),
        in_specs=[space(pltpu.VMEM)] * 4,
        out_specs=space(pltpu.VMEM),
        scratch_shapes=[pltpu.VMEM(total.shape, total.dtype)],
        compiler_params=params(),
        name="finish",
    )(total, far, tail2, tail3)


def fast_shards(psi, left_env, right_env, site_op, source):
    nsec = lax.axis_size("sec")
    nmpo = lax.axis_size("mpo")
    sdev = psi.shape[0]
    wdev = left_env.shape[0]
    blocks = jnp.transpose(psi, (0, 2, 1, 3))
    ops = site_op.astype(jnp.float32).reshape(-1)
    table = pltpu.with_memory_space_constraint(source, pltpu.HBM)
    pinned = pltpu.with_memory_space_constraint(blocks, pltpu.HBM)
    held = route(EARLY + MID + (LAST,), table, pinned)
    arrived = {0: held[0]}
    for k, value in zip(MID, held[len(EARLY) :]):
        arrived[k] = lax.ppermute(value, "sec", [(i, i ^ k) for i in range(nsec)])
    order = receive_order(table, held[0], nsec, sdev)
    both = double(held[-1], order)
    pairs = [[i, i ^ LAST] for i in range(nsec) if i < i ^ LAST]
    final = lax.all_to_all(both, "sec", 0, 0, axis_index_groups=pairs, tiled=True)

    def across(value, m):
        return lax.ppermute(value, "mpo", [(i, i ^ m) for i in range(nmpo)])

    staged = early(order, ops, [arrived[k] for k in EARLY], left_env, right_env, nsec, nmpo)
    keep, far_give, near_give = mid(order, ops, [arrived[k] for k in MID], staged, wdev, sdev)
    summed = pair(keep, across(far_give, 1), staged[6])
    far = across(summed, 2)
    near = across(near_give, 1)
    own, give1, give2, give3 = last(summed, final, staged, wdev)
    total = base(keep, near, far, own, across(give1, 1))
    out = finish(total, far, across(give2, 2), across(give3, 3))
    return jnp.transpose(out, (0, 2, 1, 3))


def any_shards(psi, left_env, right_env, site_op, source):
    me_sec = lax.axis_index("sec")
    nsec = lax.axis_size("sec")
    sdev = psi.shape[0]
    blk = psi.shape[1]
    phys = psi.shape[2]
    slots = max(2, (sdev + nsec - 1) // nsec)
    table = source[0]
    owners = (table // sdev).reshape(nsec, sdev)
    mine = owners == me_sec
    ranked = jnp.cumsum(mine.astype(jnp.int32), axis=1) - 1
    picked = mine[:, None, :] & (
        ranked[:, None, :] == jnp.arange(slots, dtype=jnp.int32)[None, :, None]
    )
    local_rows = (table % sdev).reshape(nsec, sdev)
    chosen = jnp.sum(jnp.where(picked, local_rows[:, None, :], 0), axis=2)
    outgoing = jnp.take(psi, chosen.reshape(-1), axis=0).reshape(nsec, slots, blk, phys, blk)
    arrived = lax.all_to_all(outgoing, "sec", split_axis=0, concat_axis=0, tiled=True)
    my_sources = lax.dynamic_slice_in_dim(table, me_sec * sdev, sdev)
    sender = my_sources // sdev
    onehot = (sender[:, None] == jnp.arange(nsec, dtype=jnp.int32)[None, :]).astype(jnp.int32)
    slot_index = jnp.sum(jnp.cumsum(onehot, axis=0) * onehot, axis=1) - 1
    position = sender * slots + slot_index
    taken = jnp.take(arrived.reshape(nsec * slots, blk, phys, blk), position, axis=0)
    left = jnp.einsum(
        "wtab,tbpc->wtapc", left_env, taken, preferred_element_type=jnp.float32
    ).astype(jnp.bfloat16)
    mixed = jnp.einsum(
        "wtapc,wtpq->wtaqc", left, site_op, preferred_element_type=jnp.float32
    ).astype(jnp.bfloat16)
    partial_value = jnp.einsum(
        "wtaqc,wtcd->atqd", mixed, right_env, preferred_element_type=jnp.float32
    )
    summed = lax.psum_scatter(partial_value, "mpo", scatter_dimension=0, tiled=True)
    return summed.astype(jnp.bfloat16)


def shards(psi, left_env, right_env, site_op, source):
    nsec = lax.axis_size("sec")
    nmpo = lax.axis_size("mpo")
    exact = psi.shape[0] == SLOTS * nsec and nsec == 4 and nmpo == 4
    body = fast_shards if exact else any_shards
    return body(psi, left_env, right_env, site_op, source)


def solution(mesh):
    placed = (
        P(("grp", "sec"), None, None, None),
        P(("grp", "mpo"), "sec", None, None),
        P(("grp", "mpo"), "sec", None, None),
        P(("grp", "mpo"), "sec", None, None),
        P("mpo", None),
    )
    return jax.shard_map(
        shards,
        mesh=mesh,
        in_specs=placed,
        out_specs=P("mpo", ("grp", "sec"), None, None),
        check_vma=False,
    )
```
